32 devices in a mesh: seq: 32 (over z, y, x, core).
Axes of the slice: x: 2, y: 2, z: 4, core: 2. Of those that a mesh axis runs over, the one named last changes fastest.
Arguments:
- tokens: bfloat16 [8192, 768], P('seq'), may hold values from -64 to 64
- w_query: bfloat16 [768, 768], replicated, may hold values from -0.21875 to 0.21875
- w_key: bfloat16 [768, 768], replicated, may hold values from -0.21875 to 0.21875
- w_value: bfloat16 [768, 768], replicated, may hold values from -0.21875 to 0.21875
- w_out: bfloat16 [768, 768], replicated, may hold values from -0.21875 to 0.21875
- ln_gain: float32 [768], replicated, may hold values from 0.5 to 1.5
- ln_bias: float32 [768], replicated, may hold values from -3 to 3
Outputs:
- encoded: bfloat16 [8192, 768], P('seq')
The draws below stay inside these ranges and needn't reach their ends.
All inputs are finite; a program needn't handle non-finite values.
Results may differ from the reference program's by a relative error of at most 0.003.
The reference program's roundings to bfloat16 on the way count: a program that leaves them out, or rounds other values in their place, can miss the bound.
Values may be sent and summed in bfloat16 or wider, within the bound.
A program may use at most 256 MiB of HBM per device.

```python
import math
import jax
import jax.numpy as jnp
from jax import lax

D = 768
H = 12
BLOCK = 64
NG = 128
TOK_DEV = 256
TOKENS = 8192


def draw_tokens(key, part):
    first_key = jax.random.fold_in(key, 101)
    third_key = jax.random.fold_in(key, 303)
    fourth_key = jax.random.fold_in(key, 404)
    fifth_key = jax.random.fold_in(key, 505)
    base_rows = jnp.clip(jax.random.normal(first_key, (TOKENS, D), jnp.float32), -4.0, 4.0)
    shards = TOKENS // TOK_DEV
    global_scale = 1.0
    low_strength = 10.0
    high_strength = 14.0
    row_ids = jnp.arange(TOKENS, dtype=jnp.int32)
    base_rows = base_rows * jnp.where(row_ids < NG, global_scale, 1.0)[:, None]
    device_ids = jnp.arange(shards, dtype=jnp.int32)
    targets = device_ids // 2 % NG
    places = device_ids * TOK_DEV + TOK_DEV - 1
    pair_draw = jax.random.uniform(third_key, (shards,), jnp.float32, low_strength, high_strength)
    strength = pair_draw[device_ids // 2]
    shrink = 1.0 - jnp.where(device_ids % 2 == 1, jax.random.uniform(fourth_key, (shards,), jnp.float32, 0.02, 0.08), 0.0)
    fresh_rows = jnp.clip(jax.random.normal(fifth_key, (shards, D), jnp.float32), -4.0, 4.0)
    aligned = (strength * shrink)[:, None] * base_rows[targets] + fresh_rows
    result_rows = base_rows.at[places].set(aligned)
    return jnp.clip(result_rows, -64.0, 64.0).astype(jnp.bfloat16)


def scatter_about(key, extent, scale, reach, kind=jnp.bfloat16):
    return jnp.clip(scale * jax.random.normal(key, extent, jnp.float32), -reach, reach).astype(kind)


def setup_inputs(seed: int = 0) -> dict:
    splits = jax.random.split(jax.random.key(seed), 8)
    tokens = draw_tokens(jax.random.fold_in(splits[7], 71), 0)
    w_query = scatter_about(splits[1], (D, D), D ** -0.5, 0.21875)
    w_key = scatter_about(splits[2], (D, D), D ** -0.5, 0.21875)
    w_value = scatter_about(splits[3], (D, D), D ** -0.5, 0.21875)
    w_out = scatter_about(splits[4], (D, D), D ** -0.5, 0.21875)
    ln_gain = jnp.clip(1.0 + 0.1 * jax.random.normal(splits[5], (D,), jnp.float32), 0.5, 1.5)
    ln_bias = scatter_about(splits[6], (D,), 0.5, 3.0, jnp.float32)
    return dict(tokens=tokens, w_query=w_query, w_key=w_key, w_value=w_value, w_out=w_out, ln_gain=ln_gain, ln_bias=ln_bias)


def layer_norm(summed, ln_gain, ln_bias):
    center = summed - lax.optimization_barrier(jnp.mean(summed, axis=-1, keepdims=True))
    spread = lax.optimization_barrier(jnp.mean(center * center, axis=-1, keepdims=True))
    return center * lax.rsqrt(spread + 1e-05) * ln_gain + ln_bias

def reference(tokens, w_query, w_key, w_value, w_out, ln_gain, ln_bias):
    head_dim = D // H
    factor = 1.0 / math.sqrt(head_dim)
    query_rows = jnp.dot(tokens, w_query, preferred_element_type=jnp.float32).astype(jnp.bfloat16)
    key_rows = jnp.dot(tokens, w_key, preferred_element_type=jnp.float32).astype(jnp.bfloat16)
    value_rows = jnp.dot(tokens, w_value, preferred_element_type=jnp.float32).astype(jnp.bfloat16)
    blocks = TOKENS // BLOCK
    group_size = math.gcd(blocks, 16)
    query_blocks = query_rows.reshape(blocks, BLOCK, H, head_dim)
    pad_spec = ((1, 1), (0, 0), (0, 0), (0, 0))
    key_padded = jnp.pad(key_rows.reshape(blocks, BLOCK, H, head_dim), pad_spec)
    value_padded = jnp.pad(value_rows.reshape(blocks, BLOCK, H, head_dim), pad_spec)
    global_keys = key_rows[:NG].reshape(NG, H, head_dim).astype(jnp.float32)
    global_values = value_rows[:NG].reshape(NG, H, head_dim).astype(jnp.float32)
    offsets = jnp.arange(3 * BLOCK, dtype=jnp.int32)

    def window_group(group_index):
        first_block = group_index * group_size
        query_part = lax.dynamic_slice_in_dim(query_blocks, first_block, group_size, 0).astype(jnp.float32)
        key_part = lax.dynamic_slice_in_dim(key_padded, first_block, group_size + 2, 0)
        value_part = lax.dynamic_slice_in_dim(value_padded, first_block, group_size + 2, 0)
        key_window = jnp.concatenate([key_part[:-2], key_part[1:-1], key_part[2:]], axis=1).astype(jnp.float32)
        value_window = jnp.concatenate([value_part[:-2], value_part[1:-1], value_part[2:]], axis=1).astype(jnp.float32)
        window_scores = jnp.einsum('nqhd,nkhd->nhqk', query_part, key_window) * factor
        block_ids = first_block + jnp.arange(group_size, dtype=jnp.int32)
        key_pos = block_ids[:, None] * BLOCK - BLOCK + offsets[None, :]
        usable = (key_pos >= NG) & (key_pos < TOKENS)
        window_scores = jnp.where(usable[:, None, None, :], window_scores, -jnp.inf)
        global_scores = jnp.einsum('nqhd,khd->nhqk', query_part, global_keys) * factor
        row_top = jnp.maximum(lax.optimization_barrier(jnp.max(window_scores, axis=-1)), lax.optimization_barrier(jnp.max(global_scores, axis=-1)))[..., None]
        window_exp = jnp.exp(window_scores - row_top)
        global_exp = jnp.exp(global_scores - row_top)
        row_total = lax.optimization_barrier(jnp.sum(window_exp, axis=-1)) + lax.optimization_barrier(jnp.sum(global_exp, axis=-1))
        window_weights = lax.optimization_barrier(window_exp.astype(jnp.bfloat16)).astype(jnp.float32)
        global_weights = lax.optimization_barrier(global_exp.astype(jnp.bfloat16)).astype(jnp.float32)
        blended = jnp.einsum('nhqk,nkhd->nqhd', window_weights, value_window)
        blended = blended + jnp.einsum('nhqk,khd->nqhd', global_weights, global_values)
        blended = blended / jnp.transpose(row_total, (0, 2, 1))[..., None]
        return blended.reshape(group_size * BLOCK, D).astype(jnp.bfloat16)
    attended = lax.map(window_group, jnp.arange(blocks // group_size, dtype=jnp.int32)).reshape(TOKENS, D)
    global_queries = query_rows[:NG].reshape(NG, H, head_dim).astype(jnp.float32)
    key_all = key_rows.reshape(TOKENS // TOK_DEV, TOK_DEV, H, head_dim)
    value_all = value_rows.reshape(TOKENS // TOK_DEV, TOK_DEV, H, head_dim)

    def absorb(run_state, pieces):
        run_max, run_total, run_acc = run_state
        key_piece, value_piece = pieces
        scores = jnp.einsum('ghd,jhd->hgj', global_queries, key_piece.astype(jnp.float32), precision=lax.Precision.HIGHEST) * factor
        piece_top = lax.optimization_barrier(jnp.max(scores, axis=-1))
        piece_exp = jnp.exp(scores - piece_top[..., None])
        piece_total = lax.optimization_barrier(jnp.sum(piece_exp, axis=-1))
        piece_weights = lax.optimization_barrier(piece_exp.astype(jnp.bfloat16)).astype(jnp.float32)
        piece_acc = jnp.einsum('hgj,jhd->hgd', piece_weights, value_piece.astype(jnp.float32), precision=lax.Precision.HIGHEST)
        new_max = jnp.maximum(run_max, piece_top)
        carry_decay = jnp.exp(run_max - new_max)
        piece_decay = jnp.exp(piece_top - new_max)
        run_total = run_total * carry_decay + piece_total * piece_decay
        run_acc = run_acc * carry_decay[..., None] + piece_acc * piece_decay[..., None]
        return ((new_max, run_total, run_acc), None)
    start_state = (jnp.full((H, NG), -jnp.inf, jnp.float32), jnp.zeros((H, NG), jnp.float32), jnp.zeros((H, NG, head_dim), jnp.float32))
    final_state, unused_out = lax.scan(absorb, start_state, (key_all, value_all))
    global_out = (final_state[2] / final_state[1][..., None]).transpose(1, 0, 2).reshape(NG, D)
    attended = attended.at[:NG].set(global_out.astype(jnp.bfloat16))
    projected = jnp.dot(attended, w_out, preferred_element_type=jnp.float32)
    summed = tokens.astype(jnp.float32) + projected
    return layer_norm(summed, ln_gain, ln_bias).astype(jnp.bfloat16)
```

```python
import functools
import math

import jax
import jax.numpy as jnp
from jax import lax
from jax.experimental import pallas as pl
from jax.experimental.pallas import tpu as pltpu
from jax.sharding import PartitionSpec as P

H = 12
BLOCK = 64
NG = 128
GROUP = 8
PIECE = NG // GROUP
LANES = 128
MESH = pl.DeviceIdType.MESH
BF16 = jnp.bfloat16
F32 = jnp.float32


def dot_t(a, b):
    return lax.dot_general(a, b, (((1,), (1,)), ((), ())), preferred_element_type=F32)


def kernel(
    n, tok_in, wq_in, wk_in, wv_in, wo_in, gain_ref, bias_ref, out_ref,
    tok, wq, wk, wv, wo, q, k, v, qg, mask, pacc, pst, racc, rst, cacc, cst, zacc, zst,
    piece, gout, att,
    loc, halo_s, halo_r, s1s, s1r, s2s, s2r, s3s, s3r, r1s, r1r, r2s, r2r, r3s, r3r,
):
    rows, width = tok_in.shape
    chunks = rows // NG
    pairs = width // LANES
    groups = n // GROUP
    scale = 1.0 / math.sqrt(width // H)
    own = BLOCK
    right_at = BLOCK + rows
    glob = rows + 2 * BLOCK
    me = lax.axis_index("seq")
    g = me // GROUP
    j = me % GROUP
    base = g * GROUP

    def remote(src, dst, ss, rs, dev):
        return pltpu.make_async_remote_copy(
            src_ref=src, dst_ref=dst, send_sem=ss, recv_sem=rs, device_id=(dev,), device_id_type=MESH
        )

    local = [
        pltpu.make_async_copy(tok_in, tok.at[pl.ds(own, rows)], loc.at[0]),
        pltpu.make_async_copy(wq_in, wq, loc.at[1]),
        pltpu.make_async_copy(wk_in, wk, loc.at[2]),
        pltpu.make_async_copy(wv_in, wv, loc.at[3]),
        pltpu.make_async_copy(wo_in, wo, loc.at[4]),
    ]
    for copy in local:
        copy.start()

    barrier = pltpu.get_barrier_semaphore()

    def greet(dev):
        pl.semaphore_signal(barrier, inc=1, device_id=(dev,), device_id_type=MESH)

    for d in range(1, GROUP):
        greet(base + (j + d) % GROUP)

    @pl.when(g == 0)
    def _():
        for other in range(1, groups):
            greet(other * GROUP + j)

    @pl.when(g > 0)
    def _():
        greet(j)

    has_left = me > 0
    has_right = me < n - 1
    cross_left = (j == 0) & (g > 0)
    cross_right = (j == GROUP - 1) & (g < groups - 1)

    @pl.when(cross_left)
    def _():
        greet(me - 1)

    @pl.when(cross_right)
    def _():
        greet(me + 1)

    peers = GROUP - 1 + jnp.where(g == 0, groups - 1, 1) + jnp.where(cross_left, 1, 0) + jnp.where(cross_right, 1, 0)
    pl.semaphore_wait(barrier, peers)

    def glob_piece(index):
        return tok.at[pl.ds(pl.multiple_of(glob + index * PIECE, PIECE), PIECE)]

    def scatter(d):
        return remote(tok_in.at[pl.ds(d * PIECE, PIECE)], glob_piece(d), s1s.at[d], s1r.at[0], d)

    def climb(other):
        return remote(glob_piece(j), glob_piece(j), s2s.at[other], s2r.at[0], other * GROUP + j)

    def gather(d):
        t = (j + d) % GROUP
        return remote(glob_piece(j), glob_piece(j), s3s.at[d], s3r.at[d], base + t)

    keep = pltpu.make_async_copy(tok_in.at[pl.ds(0, NG)], tok.at[pl.ds(glob, NG)], loc.at[5])

    @pl.when(me == 0)
    def _():
        for d in range(1, GROUP):
            scatter(d).start()
        keep.start()

    to_left = remote(tok_in.at[pl.ds(0, BLOCK)], tok.at[pl.ds(right_at, BLOCK)], halo_s.at[0], halo_r.at[0], me - 1)
    to_right = remote(
        tok_in.at[pl.ds(rows - BLOCK, BLOCK)], tok.at[pl.ds(0, BLOCK)], halo_s.at[1], halo_r.at[1], me + 1
    )

    @pl.when(has_left)
    def _():
        to_left.start()

    @pl.when(has_right)
    def _():
        to_right.start()

    @pl.when(me == 0)
    def _():
        tok[0:BLOCK] = jnp.zeros((BLOCK, width), BF16)

    @pl.when(me == n - 1)
    def _():
        tok[right_at : right_at + BLOCK] = jnp.zeros((BLOCK, width), BF16)

    tile = 2 * LANES if width % (2 * LANES) == 0 else LANES

    def project(start, count, w, dst):
        @pl.loop(0, width // tile)
        def _(t):
            cols = pl.ds(pl.multiple_of(t * tile, tile), tile)
            dst[start : start + count, cols] = jnp.dot(
                tok[start : start + count], w[:, cols], preferred_element_type=F32
            ).astype(BF16)

    def project_query(start, count, dst):
        first_half = lax.broadcasted_iota(jnp.int32, (NG, tile), 1) % LANES < BLOCK

        @pl.loop(0, width // tile)
        def _(t):
            cols = pl.ds(pl.multiple_of(t * tile, tile), tile)
            res = jnp.dot(tok[start : start + count], wq[:, cols], preferred_element_type=F32) * scale
            for c in range(count // NG):
                part = res[c * NG : (c + 1) * NG]
                dst[2 * c * NG : (2 * c + 1) * NG, cols] = jnp.where(first_half, part, 0.0).astype(BF16)
                dst[(2 * c + 1) * NG : (2 * c + 2) * NG, cols] = jnp.where(first_half, 0.0, part).astype(BF16)

    local[0].wait()
    local[1].wait()
    project_query(own, rows, q)

    def gather_sends():
        for d in range(1, GROUP):
            @pl.when((g > 0) | ((j + d) % GROUP != 0))
            def _():
                gather(d).start()

    @pl.when(g == 0)
    def _():
        @pl.when(j > 0)
        def _():
            remote(glob_piece(j), glob_piece(j), s1s.at[0], s1r.at[0], 0).wait_recv()

        @pl.when(j == 0)
        def _():
            keep.wait()

        for other in range(1, groups):
            climb(other).start()
        gather_sends()

    local[2].wait()
    project(own, rows, wk, k)

    @pl.when(g > 0)
    def _():
        remote(glob_piece(j), glob_piece(j), s2s.at[0], s2r.at[0], j).wait_recv()
        gather_sends()

    local[3].wait()
    project(own, rows, wv, v)

    shape = (2 * NG, NG + 2 * BLOCK)
    row_block = lax.broadcasted_iota(jnp.int32, shape, 0) % NG // BLOCK
    key_id = lax.broadcasted_iota(jnp.int32, shape, 1)
    apart = key_id // BLOCK - row_block
    for c in range(chunks):
        place = me * rows + (c * NG - BLOCK) + key_id
        ok = (apart >= 0) & (apart <= 2) & (place >= NG) & (place < n * rows)
        mask[c] = jnp.where(ok, 0.0, -jnp.inf).astype(F32)

    @pl.when(me > 0)
    def _():
        for d in range(1, GROUP):
            t = (j + GROUP - d) % GROUP
            remote(glob_piece(t), glob_piece(t), s3s.at[d], s3r.at[d], base + t).wait_recv()

    project_query(glob, NG, qg)

    lane = lax.broadcasted_iota(jnp.int32, (NG, LANES), 1)
    low = lane < BLOCK
    pst[...] = jnp.zeros((NG, LANES), F32)

    @pl.loop(0, pairs)
    def _(p):
        cols = pl.ds(pl.multiple_of(p * LANES, LANES), LANES)
        s = dot_t(qg[:, cols], k[own : own + rows, cols])
        top = jnp.max(s, axis=-1, keepdims=True)
        e = jnp.exp(s - top)
        total = jnp.sum(e, axis=-1, keepdims=True)
        o = jnp.dot(e.astype(BF16), v[own : own + rows, cols], preferred_element_type=F32)
        pacc[:, cols] = jnp.where(low, o[:NG], o[NG:]).astype(BF16)
        st = pst[...]
        st = jnp.where(lane == 2 * p, top[:NG], st)
        st = jnp.where(lane == 2 * p + 1, top[NG:], st)
        st = jnp.where(lane == BLOCK + 2 * p, total[:NG], st)
        st = jnp.where(lane == BLOCK + 2 * p + 1, total[NG:], st)
        pst[...] = st

    def part(index):
        return pl.ds(pl.multiple_of(index * PIECE, PIECE), PIECE)

    def spread(d):
        t = (j + d) % GROUP
        return (
            remote(pacc.at[part(t)], racc.at[d], r1s.at[0, d], r1r.at[0, d], base + t),
            remote(pst.at[part(t)], rst.at[d], r1s.at[1, d], r1r.at[1, d], base + t),
        )

    for d in range(1, GROUP):
        for copy in spread(d):
            copy.start()
    racc[0] = pacc[part(j)]
    rst[0] = pst[part(j)]

    small_lane = lax.broadcasted_iota(jnp.int32, (PIECE, LANES), 1)
    small_low = small_lane < BLOCK

    def per_head(x, p, offset):
        return jnp.where(
            small_low, x[:, offset + 2 * p : offset + 2 * p + 1], x[:, offset + 2 * p + 1 : offset + 2 * p + 2]
        )

    def combine(count, accs, sts):
        st = [sts[d] for d in range(count)]
        top = functools.reduce(jnp.maximum, st)
        factors = [jnp.exp(s - top) for s in st]
        total = sum(pltpu.roll(f, BLOCK, 1) * s for f, s in zip(factors, st))
        sums = []
        for p in range(pairs):
            cols = slice(p * LANES, (p + 1) * LANES)
            sums.append(sum(per_head(factors[d], p, 0) * accs[d, :, cols].astype(F32) for d in range(count)))
        return sums, jnp.where(small_low, top, total)

    def window(c, p):
        cols = pl.ds(pl.multiple_of(p * LANES, LANES), LANES)
        span = slice(c * NG, c * NG + NG + 2 * BLOCK)
        qs = q[2 * c * NG : 2 * (c + 1) * NG, cols]
        sw = dot_t(qs, k[span, cols]) + mask[c]
        sg = dot_t(qs, k[glob : glob + NG, cols])
        top = jnp.maximum(jnp.max(sw, axis=-1, keepdims=True), jnp.max(sg, axis=-1, keepdims=True))
        ew = jnp.exp(sw - top)
        eg = jnp.exp(sg - top)
        total = jnp.sum(ew, axis=-1, keepdims=True) + jnp.sum(eg, axis=-1, keepdims=True)
        o = jnp.dot(ew.astype(BF16), v[span, cols], preferred_element_type=F32)
        o = o + jnp.dot(eg.astype(BF16), v[glob : glob + NG, cols], preferred_element_type=F32)
        o = o / total
        att[c * NG : (c + 1) * NG, cols] = jnp.where(low, o[:NG], o[NG:]).astype(BF16)

    def windows(c, first, last):
        @pl.loop(first, last)
        def _(p):
            window(c, p)

    def finish(c):
        at = slice(c * NG, (c + 1) * NG)
        proj = jnp.dot(att[at], wo[...], preferred_element_type=F32)
        summed = tok[own + c * NG : own + (c + 1) * NG].astype(F32) + proj
        center = summed - jnp.mean(summed, axis=-1, keepdims=True)
        spread_ = jnp.mean(center * center, axis=-1, keepdims=True)
        out_ref[at] = (center * lax.rsqrt(spread_ + 1e-05) * gain_ref[...] + bias_ref[...]).astype(BF16)

    @pl.when(has_left)
    def _():
        to_right.wait_recv()

    @pl.when(has_right)
    def _():
        to_left.wait_recv()

    for w, dst in ((wk, k), (wv, v)):
        project(0, BLOCK, w, dst)
        project(right_at, BLOCK + NG, w, dst)

    half = pairs // 2
    last = chunks - 1
    windows(last, 0, half)

    for d in range(1, GROUP):
        for copy in spread(d):
            copy.wait_recv()
    sums, st = combine(GROUP, racc, rst)

    @pl.when(g == 0)
    def _():
        for p in range(pairs):
            zacc[0, :, p * LANES : (p + 1) * LANES] = sums[p].astype(BF16)
        zst[0] = st

    def raise_up():
        return (
            remote(cacc, zacc.at[g], r2s.at[0], r2r.at[0, g], j),
            remote(cst, zst.at[g], r2s.at[1], r2r.at[1, g], j),
        )

    @pl.when(g > 0)
    def _():
        for p in range(pairs):
            cacc[:, p * LANES : (p + 1) * LANES] = sums[p].astype(BF16)
        cst[...] = st
        for copy in raise_up():
            copy.start()

    windows(last, half, pairs)
    for c in range(last):
        windows(c, 0, half)

    deliver = remote(piece, gout.at[part(j)], r3s.at[0], r3r.at[j], 0)

    @pl.when(g == 0)
    def _():
        for other in range(1, groups):
            remote(cacc, zacc.at[other], r2s.at[0], r2r.at[0, other], other * GROUP + j).wait_recv()
            remote(cst, zst.at[other], r2s.at[1], r2r.at[1, other], other * GROUP + j).wait_recv()
        full, full_st = combine(groups, zacc, zst)
        for p in range(pairs):
            piece[:, p * LANES : (p + 1) * LANES] = (full[p] / per_head(full_st, p, BLOCK)).astype(BF16)

        @pl.when(j > 0)
        def _():
            deliver.start()

        @pl.when(j == 0)
        def _():
            gout[0:PIECE] = piece[...]

    for c in range(last):
        windows(c, half, pairs)
    local[4].wait()
    for c in range(1, chunks):
        finish(c)

    @pl.when(me == 0)
    def _():
        for d in range(1, GROUP):
            remote(piece, gout.at[pl.ds(d * PIECE, PIECE)], r3s.at[0], r3r.at[d], d).wait_recv()
        att[0:NG] = gout[...]

    finish(0)

    @pl.when(has_left)
    def _():
        to_left.wait_send()

    @pl.when(has_right)
    def _():
        to_right.wait_send()

    @pl.when(me == 0)
    def _():
        for d in range(1, GROUP):
            scatter(d).wait_send()

    @pl.when(g == 0)
    def _():
        for other in range(1, groups):
            climb(other).wait_send()

        @pl.when(j > 0)
        def _():
            deliver.wait_send()

    @pl.when(g > 0)
    def _():
        for copy in raise_up():
            copy.wait_send()

    for d in range(1, GROUP):
        @pl.when((g > 0) | ((j + d) % GROUP != 0))
        def _():
            gather(d).wait_send()

        for copy in spread(d):
            copy.wait_send()


def shards(n, tokens, w_query, w_key, w_value, w_out, ln_gain, ln_bias):
    rows, width = tokens.shape
    groups = n // GROUP
    ext = rows + 2 * BLOCK + NG
    dma = pltpu.SemaphoreType.DMA
    weight = pltpu.VMEM((width, width), BF16)
    scratch = [
        pltpu.VMEM((ext, width), BF16),
        weight, weight, weight, weight,
        pltpu.VMEM((2 * rows, width), BF16),
        pltpu.VMEM((ext, width), BF16),
        pltpu.VMEM((ext, width), BF16),
        pltpu.VMEM((2 * NG, width), BF16),
        pltpu.VMEM((rows // NG, 2 * NG, NG + 2 * BLOCK), F32),
        pltpu.VMEM((NG, width), BF16),
        pltpu.VMEM((NG, LANES), F32),
        pltpu.VMEM((GROUP, PIECE, width), BF16),
        pltpu.VMEM((GROUP, PIECE, LANES), F32),
        pltpu.VMEM((PIECE, width), BF16),
        pltpu.VMEM((PIECE, LANES), F32),
        pltpu.VMEM((groups, PIECE, width), BF16),
        pltpu.VMEM((groups, PIECE, LANES), F32),
        pltpu.VMEM((PIECE, width), BF16),
        pltpu.VMEM((NG, width), BF16),
        pltpu.VMEM((rows, width), BF16),
        dma((6,)), dma((2,)), dma((2,)),
        dma((GROUP,)), dma((1,)),
        dma((groups,)), dma((1,)),
        dma((GROUP,)), dma((GROUP,)),
        dma((2, GROUP)), dma((2, GROUP)),
        dma((2,)), dma((2, groups)),
        dma((1,)), dma((GROUP,)),
    ]
    anywhere = pl.BlockSpec(memory_space=pl.ANY)
    vmem = pl.BlockSpec(memory_space=pltpu.VMEM)
    return pl.pallas_call(
        functools.partial(kernel, n),
        out_shape=jax.ShapeDtypeStruct((rows, width), BF16),
        in_specs=[anywhere] * 5 + [vmem] * 2,
        out_specs=vmem,
        scratch_shapes=scratch,
        compiler_params=pltpu.CompilerParams(
            collective_id=0, has_side_effects=True, vmem_limit_bytes=40 * 1024 * 1024
        ),
    )(tokens, w_query, w_key, w_value, w_out, ln_gain.reshape(1, width), ln_bias.reshape(1, width))


def solution(mesh):
    n = mesh.shape["seq"]
    in_specs = (P("seq", None), P(), P(), P(), P(), P(), P())
    return jax.shard_map(
        functools.partial(shards, n), mesh=mesh, in_specs=in_specs, out_specs=P("seq", None), check_vma=False
    )
```

```python
import functools
import math

import jax
import jax.numpy as jnp
from jax import lax
from jax.experimental import pallas as pl
from jax.experimental.pallas import tpu as pltpu
from jax.sharding import PartitionSpec as P

H = 12
BLOCK = 64
NG = 128
GROUP = 8
PIECE = NG // GROUP
LANES = 128
MESH = pl.DeviceIdType.MESH
BF16 = jnp.bfloat16
F32 = jnp.float32


def dot_t(a, b):
    return lax.dot_general(a, b, (((1,), (1,)), ((), ())), preferred_element_type=F32)


def kernel(
    n, tok_in, wq_in, wk_in, wv_in, wo_in, gain_in, bias_in, out_ref,
    tok, wq, wk, wv, wo, gain_ref, bias_ref, q, k, v, qg, mask, pacc, pst, racc, cacc, zacc,
    piece, gout, att,
    loc, halo_s, halo_r, s1s, s1r, s2s, s2r, s3s, s3r, r1s, r1r, r2s, r2r, r3s, r3r,
):
    rows, width = tok_in.shape
    chunks = rows // NG
    pairs = width // LANES
    groups = n // GROUP
    scale = 1.0 / math.sqrt(width // H)
    own = BLOCK
    right_at = BLOCK + rows
    glob = rows + 2 * BLOCK
    me = lax.axis_index("seq")
    g = me // GROUP
    j = me % GROUP
    base = g * GROUP

    def remote(src, dst, ss, rs, dev):
        return pltpu.make_async_remote_copy(
            src_ref=src, dst_ref=dst, send_sem=ss, recv_sem=rs, device_id=(dev,), device_id_type=MESH
        )

    local = [
        pltpu.make_async_copy(tok_in, tok.at[pl.ds(own, rows)], loc.at[0]),
        pltpu.make_async_copy(wq_in, wq, loc.at[1]),
        pltpu.make_async_copy(wk_in, wk, loc.at[2]),
        pltpu.make_async_copy(wv_in, wv, loc.at[3]),
        pltpu.make_async_copy(wo_in, wo, loc.at[4]),
        pltpu.make_async_copy(gain_in, gain_ref, loc.at[6]),
        pltpu.make_async_copy(bias_in, bias_ref, loc.at[7]),
    ]
    for copy in local[:2]:
        copy.start()

    barrier = pltpu.get_barrier_semaphore()

    def greet(dev):
        pl.semaphore_signal(barrier, inc=1, device_id=(dev,), device_id_type=MESH)

    for d in range(1, GROUP):
        greet(base + (j + d) % GROUP)

    @pl.when(g == 0)
    def _():
        for other in range(1, groups):
            greet(other * GROUP + j)

    @pl.when(g > 0)
    def _():
        greet(j)

    has_left = me > 0
    has_right = me < n - 1
    cross_left = (j == 0) & (g > 0)
    cross_right = (j == GROUP - 1) & (g < groups - 1)

    @pl.when(cross_left)
    def _():
        greet(me - 1)

    @pl.when(cross_right)
    def _():
        greet(me + 1)

    peers = GROUP - 1 + jnp.where(g == 0, groups - 1, 1) + jnp.where(cross_left, 1, 0) + jnp.where(cross_right, 1, 0)
    pl.semaphore_wait(barrier, peers)

    def glob_piece(index):
        return tok.at[pl.ds(pl.multiple_of(glob + index * PIECE, PIECE), PIECE)]

    def scatter(d):
        return remote(tok_in.at[pl.ds(d * PIECE, PIECE)], glob_piece(d), s1s.at[d], s1r.at[0], d)

    def climb(other):
        return remote(glob_piece(j), glob_piece(j), s2s.at[other], s2r.at[0], other * GROUP + j)

    def gather(d):
        t = (j + d) % GROUP
        return remote(glob_piece(j), glob_piece(j), s3s.at[d], s3r.at[d], base + t)

    keep = pltpu.make_async_copy(tok_in.at[pl.ds(0, NG)], tok.at[pl.ds(glob, NG)], loc.at[5])

    @pl.when(me == 0)
    def _():
        for d in range(1, GROUP):
            scatter(d).start()
        keep.start()

    to_left = remote(tok_in.at[pl.ds(0, BLOCK)], tok.at[pl.ds(right_at, BLOCK)], halo_s.at[0], halo_r.at[0], me - 1)
    to_right = remote(
        tok_in.at[pl.ds(rows - BLOCK, BLOCK)], tok.at[pl.ds(0, BLOCK)], halo_s.at[1], halo_r.at[1], me + 1
    )

    @pl.when(has_left)
    def _():
        to_left.start()

    @pl.when(has_right)
    def _():
        to_right.start()

    for copy in local[2:]:
        copy.start()

    @pl.when(me == 0)
    def _():
        tok[0:BLOCK] = jnp.zeros((BLOCK, width), BF16)

    @pl.when(me == n - 1)
    def _():
        tok[right_at : right_at + BLOCK] = jnp.zeros((BLOCK, width), BF16)

    tile = 2 * LANES if width % (2 * LANES) == 0 else LANES

    def project(start, count, w, dst):
        @pl.loop(0, width // tile)
        def _(t):
            cols = pl.ds(pl.multiple_of(t * tile, tile), tile)
            dst[start : start + count, cols] = jnp.dot(
                tok[start : start + count], w[:, cols], preferred_element_type=F32
            ).astype(BF16)

    def project_query(start, count, dst):
        first_half = lax.broadcasted_iota(jnp.int32, (NG, tile), 1) % LANES < BLOCK

        @pl.loop(0, width // tile)
        def _(t):
            cols = pl.ds(pl.multiple_of(t * tile, tile), tile)
            res = jnp.dot(tok[start : start + count], wq[:, cols], preferred_element_type=F32) * scale
            for c in range(count // NG):
                part = res[c * NG : (c + 1) * NG]
                dst[2 * c * NG : (2 * c + 1) * NG, cols] = jnp.where(first_half, part, 0.0).astype(BF16)
                dst[(2 * c + 1) * NG : (2 * c + 2) * NG, cols] = jnp.where(first_half, 0.0, part).astype(BF16)

    local[0].wait()
    local[1].wait()
    project_query(own, rows, q)

    def gather_sends():
        for d in range(1, GROUP):
            @pl.when((g > 0) | ((j + d) % GROUP != 0))
            def _():
                gather(d).start()

    @pl.when(g == 0)
    def _():
        @pl.when(j > 0)
        def _():
            remote(glob_piece(j), glob_piece(j), s1s.at[0], s1r.at[0], 0).wait_recv()

        @pl.when(j == 0)
        def _():
            keep.wait()

        for other in range(1, groups):
            climb(other).start()
        gather_sends()

    local[2].wait()
    project(own, rows, wk, k)

    @pl.when(g > 0)
    def _():
        remote(glob_piece(j), glob_piece(j), s2s.at[0], s2r.at[0], j).wait_recv()
        gather_sends()

    local[3].wait()
    project(own, rows, wv, v)

    shape = (2 * NG, NG + 2 * BLOCK)
    row_block = lax.broadcasted_iota(jnp.int32, shape, 0) % NG // BLOCK
    key_id = lax.broadcasted_iota(jnp.int32, shape, 1)
    apart = key_id // BLOCK - row_block
    for c in range(chunks):
        place = me * rows + (c * NG - BLOCK) + key_id
        ok = (apart >= 0) & (apart <= 2) & (place >= NG) & (place < n * rows)
        mask[c] = jnp.where(ok, 0.0, -jnp.inf).astype(F32)

    @pl.when(me > 0)
    def _():
        for d in range(1, GROUP):
            t = (j + GROUP - d) % GROUP
            remote(glob_piece(t), glob_piece(t), s3s.at[d], s3r.at[d], base + t).wait_recv()

    project_query(glob, NG, qg)

    lane = lax.broadcasted_iota(jnp.int32, (NG, LANES), 1)
    low = lane < BLOCK
    pst[...] = jnp.zeros((NG, LANES), F32)

    @pl.loop(0, pairs)
    def _(p):
        cols = pl.ds(pl.multiple_of(p * LANES, LANES), LANES)
        s = dot_t(qg[:, cols], k[own : own + rows, cols])
        top = jnp.max(s, axis=-1, keepdims=True)
        e = jnp.exp(s - top)
        total = jnp.sum(e, axis=-1, keepdims=True)
        o = jnp.dot(e.astype(BF16), v[own : own + rows, cols], preferred_element_type=F32)
        pacc[:, cols] = jnp.where(low, o[:NG], o[NG:]).astype(BF16)
        st = pst[...]
        st = jnp.where(lane == 2 * p, top[:NG], st)
        st = jnp.where(lane == 2 * p + 1, top[NG:], st)
        st = jnp.where(lane == BLOCK + 2 * p, total[:NG], st)
        st = jnp.where(lane == BLOCK + 2 * p + 1, total[NG:], st)
        pst[...] = st

    def part(index):
        return pl.ds(pl.multiple_of(index * PIECE, PIECE), PIECE)

    def encode(x):
        hi = x.astype(BF16)
        rest = x - hi.astype(F32)
        mid = rest.astype(BF16)
        lo = (rest - mid.astype(F32)).astype(BF16)
        return (
            hi.astype(F32) + pltpu.roll(mid.astype(F32), 16, 1) + pltpu.roll(lo.astype(F32), 32, 1)
        ).astype(BF16)

    def decode(x):
        x = x.astype(F32)
        return x + pltpu.roll(x, LANES - 16, 1) + pltpu.roll(x, LANES - 32, 1)

    pacc[:, width:] = encode(pst[...])

    def spread(d):
        t = (j + d) % GROUP
        return remote(pacc.at[part(t)], racc.at[d], r1s.at[d], r1r.at[d], base + t)

    for d in range(1, GROUP):
        spread(d).start()
    racc[0] = pacc[part(j)]

    small_lane = lax.broadcasted_iota(jnp.int32, (PIECE, LANES), 1)
    small_low = small_lane < BLOCK

    def per_head(x, p, offset):
        return jnp.where(
            small_low, x[:, offset + 2 * p : offset + 2 * p + 1], x[:, offset + 2 * p + 1 : offset + 2 * p + 2]
        )

    def combine(count, accs):
        st = [decode(accs[d, :, width:]) for d in range(count)]
        top = functools.reduce(jnp.maximum, st)
        factors = [jnp.exp(s - top) for s in st]
        total = sum(pltpu.roll(f, BLOCK, 1) * s for f, s in zip(factors, st))
        sums = []
        for p in range(pairs):
            cols = slice(p * LANES, (p + 1) * LANES)
            sums.append(sum(per_head(factors[d], p, 0) * accs[d, :, cols].astype(F32) for d in range(count)))
        st = jnp.where(small_low, top, total)
        return sums, jnp.where(small_lane % BLOCK < H, st, 0.0)

    def window(c, p):
        cols = pl.ds(pl.multiple_of(p * LANES, LANES), LANES)
        span = slice(c * NG, c * NG + NG + 2 * BLOCK)
        qs = q[2 * c * NG : 2 * (c + 1) * NG, cols]
        sw = dot_t(qs, k[span, cols]) + mask[c]
        sg = dot_t(qs, k[glob : glob + NG, cols])
        top = jnp.maximum(jnp.max(sw, axis=-1, keepdims=True), jnp.max(sg, axis=-1, keepdims=True))
        ew = jnp.exp(sw - top)
        eg = jnp.exp(sg - top)
        total = jnp.sum(ew, axis=-1, keepdims=True) + jnp.sum(eg, axis=-1, keepdims=True)
        o = jnp.dot(ew.astype(BF16), v[span, cols], preferred_element_type=F32)
        o = o + jnp.dot(eg.astype(BF16), v[glob : glob + NG, cols], preferred_element_type=F32)
        o = o / total
        att[c * NG : (c + 1) * NG, cols] = jnp.where(low, o[:NG], o[NG:]).astype(BF16)

    def windows(c, first, last):
        @pl.loop(first, last)
        def _(p):
            window(c, p)

    def finish(c):
        at = slice(c * NG, (c + 1) * NG)
        proj = jnp.dot(att[at], wo[...], preferred_element_type=F32)
        summed = tok[own + c * NG : own + (c + 1) * NG].astype(F32) + proj
        center = summed - jnp.mean(summed, axis=-1, keepdims=True)
        spread_ = jnp.mean(center * center, axis=-1, keepdims=True)
        out_ref[at] = (center * lax.rsqrt(spread_ + 1e-05) * gain_ref[...][None] + bias_ref[...][None]).astype(BF16)

    @pl.when(has_left)
    def _():
        to_right.wait_recv()

    @pl.when(has_right)
    def _():
        to_left.wait_recv()

    for w, dst in ((wk, k), (wv, v)):
        project(0, BLOCK, w, dst)
        project(right_at, BLOCK + NG, w, dst)

    half = pairs // 2
    last = chunks - 1
    windows(last, 0, half)

    for d in range(1, GROUP):
        spread(d).wait_recv()
    sums, st = combine(GROUP, racc)

    def pack(dst, slot):
        for p in range(pairs):
            dst[slot, :, p * LANES : (p + 1) * LANES] = sums[p].astype(BF16)
        dst[slot, :, width:] = encode(st)

    raise_up = remote(cacc.at[0], zacc.at[g], r2s.at[0], r2r.at[g], j)

    @pl.when(g == 0)
    def _():
        pack(zacc, 0)

    @pl.when(g > 0)
    def _():
        pack(cacc, 0)
        raise_up.start()

    windows(last, half, pairs)
    for c in range(last):
        windows(c, 0, half)

    deliver = remote(piece, gout.at[part(j)], r3s.at[0], r3r.at[j], 0)

    @pl.when(g == 0)
    def _():
        for other in range(1, groups):
            remote(cacc.at[0], zacc.at[other], r2s.at[0], r2r.at[other], other * GROUP + j).wait_recv()
        full, full_st = combine(groups, zacc)
        for p in range(pairs):
            piece[:, p * LANES : (p + 1) * LANES] = (full[p] / per_head(full_st, p, BLOCK)).astype(BF16)

        @pl.when(j > 0)
        def _():
            deliver.start()

        @pl.when(j == 0)
        def _():
            gout[0:PIECE] = piece[...]

    for c in range(last):
        windows(c, half, pairs)
    for copy in local[4:]:
        copy.wait()
    for c in range(1, chunks):
        finish(c)

    @pl.when(me == 0)
    def _():
        for d in range(1, GROUP):
            remote(piece, gout.at[pl.ds(d * PIECE, PIECE)], r3s.at[0], r3r.at[d], d).wait_recv()
        att[0:NG] = gout[...]

    finish(0)

    @pl.when(has_left)
    def _():
        to_left.wait_send()

    @pl.when(has_right)
    def _():
        to_right.wait_send()

    @pl.when(me == 0)
    def _():
        for d in range(1, GROUP):
            scatter(d).wait_send()

    @pl.when(g == 0)
    def _():
        for other in range(1, groups):
            climb(other).wait_send()

        @pl.when(j > 0)
        def _():
            deliver.wait_send()

    @pl.when(g > 0)
    def _():
        raise_up.wait_send()

    for d in range(1, GROUP):
        @pl.when((g > 0) | ((j + d) % GROUP != 0))
        def _():
            gather(d).wait_send()

        spread(d).wait_send()


def shards(n, tokens, w_query, w_key, w_value, w_out, ln_gain, ln_bias):
    rows, width = tokens.shape
    groups = n // GROUP
    ext = rows + 2 * BLOCK + NG
    dma = pltpu.SemaphoreType.DMA
    weight = pltpu.VMEM((width, width), BF16)
    scratch = [
        pltpu.VMEM((ext, width), BF16),
        weight, weight, weight, weight,
        pltpu.VMEM((width,), F32),
        pltpu.VMEM((width,), F32),
        pltpu.VMEM((2 * rows, width), BF16),
        pltpu.VMEM((ext, width), BF16),
        pltpu.VMEM((ext, width), BF16),
        pltpu.VMEM((2 * NG, width), BF16),
        pltpu.VMEM((rows // NG, 2 * NG, NG + 2 * BLOCK), F32),
        pltpu.VMEM((NG, width + LANES), BF16),
        pltpu.VMEM((NG, LANES), F32),
        pltpu.VMEM((GROUP, PIECE, width + LANES), BF16),
        pltpu.VMEM((1, PIECE, width + LANES), BF16),
        pltpu.VMEM((groups, PIECE, width + LANES), BF16),
        pltpu.VMEM((PIECE, width), BF16),
        pltpu.VMEM((NG, width), BF16),
        pltpu.VMEM((rows, width), BF16),
        dma((8,)), dma((2,)), dma((2,)),
        dma((GROUP,)), dma((1,)),
        dma((groups,)), dma((1,)),
        dma((GROUP,)), dma((GROUP,)),
        dma((GROUP,)), dma((GROUP,)),
        dma((1,)), dma((groups,)),
        dma((1,)), dma((GROUP,)),
    ]
    anywhere = pl.BlockSpec(memory_space=pl.ANY)
    vmem = pl.BlockSpec(memory_space=pltpu.VMEM)
    return pl.pallas_call(
        functools.partial(kernel, n),
        out_shape=jax.ShapeDtypeStruct((rows, width), BF16),
        in_specs=[anywhere] * 7,
        out_specs=vmem,
        scratch_shapes=scratch,
        compiler_params=pltpu.CompilerParams(
            collective_id=0, has_side_effects=True, vmem_limit_bytes=60 * 1024 * 1024
        ),
    )(tokens, w_query, w_key, w_value, w_out, ln_gain, ln_bias)


def solution(mesh):
    n = mesh.shape["seq"]
    in_specs = (P("seq", None), P(), P(), P(), P(), P(), P())
    return jax.shard_map(
        functools.partial(shards, n), mesh=mesh, in_specs=in_specs, out_specs=P("seq", None), check_vma=False
    )
```

```python
import functools
import math

import jax
import jax.numpy as jnp
from jax import lax
from jax.experimental import pallas as pl
from jax.experimental.pallas import tpu as pltpu
from jax.sharding import PartitionSpec as P

H = 12
BLOCK = 64
NG = 128
GROUP = 8
PIECE = NG // GROUP
LANES = 128
MESH = pl.DeviceIdType.MESH
BF16 = jnp.bfloat16
F32 = jnp.float32


def dot_t(a, b):
    return lax.dot_general(a, b, (((1,), (1,)), ((), ())), preferred_element_type=F32)


def kernel(
    n, tok_in, wq_in, wk_in, wv_in, wo_in, gain_in, bias_in, out_ref,
    tok, wq, wk, wv, wo, gain_ref, bias_ref, q, k, v, qg, mask, pacc, racc, cacc, zacc,
    piece, gout, att,
    loc, halo_s, halo_r, s1s, s1r, s2s, s2r, s3s, s3r, r1s, r1r, r2s, r2r, r3s, r3r,
):
    rows, width = tok_in.shape
    chunks = rows // NG
    pairs = width // LANES
    groups = n // GROUP
    scale = 1.0 / math.sqrt(width // H)
    own = BLOCK
    right_at = BLOCK + rows
    glob = rows + 2 * BLOCK
    me = lax.axis_index("seq")
    g = me // GROUP
    j = me % GROUP
    base = g * GROUP

    def remote(src, dst, ss, rs, dev):
        return pltpu.make_async_remote_copy(
            src_ref=src, dst_ref=dst, send_sem=ss, recv_sem=rs, device_id=(dev,), device_id_type=MESH
        )

    local = [
        pltpu.make_async_copy(tok_in, tok.at[pl.ds(own, rows)], loc.at[0]),
        pltpu.make_async_copy(wq_in, wq, loc.at[1]),
        pltpu.make_async_copy(wk_in, wk, loc.at[2]),
        pltpu.make_async_copy(wv_in, wv, loc.at[3]),
        pltpu.make_async_copy(wo_in, wo, loc.at[4]),
        pltpu.make_async_copy(gain_in, gain_ref, loc.at[6]),
        pltpu.make_async_copy(bias_in, bias_ref, loc.at[7]),
    ]
    for copy in local[:2]:
        copy.start()

    barrier = pltpu.get_barrier_semaphore()

    def greet(dev):
        pl.semaphore_signal(barrier, inc=1, device_id=(dev,), device_id_type=MESH)

    for d in range(1, GROUP):
        greet(base + (j + d) % GROUP)

    @pl.when(g == 0)
    def _():
        for other in range(1, groups):
            greet(other * GROUP + j)

    @pl.when(g > 0)
    def _():
        greet(j)

    has_left = me > 0
    has_right = me < n - 1
    cross_left = (j == 0) & (g > 0)
    cross_right = (j == GROUP - 1) & (g < groups - 1)

    @pl.when(cross_left)
    def _():
        greet(me - 1)

    @pl.when(cross_right)
    def _():
        greet(me + 1)

    peers = GROUP - 1 + jnp.where(g == 0, groups - 1, 1) + jnp.where(cross_left, 1, 0) + jnp.where(cross_right, 1, 0)
    pl.semaphore_wait(barrier, peers)

    def glob_piece(index):
        return tok.at[pl.ds(pl.multiple_of(glob + index * PIECE, PIECE), PIECE)]

    def scatter(d):
        return remote(tok_in.at[pl.ds(d * PIECE, PIECE)], glob_piece(d), s1s.at[d], s1r.at[0], d)

    def climb(other):
        return remote(glob_piece(j), glob_piece(j), s2s.at[other], s2r.at[0], other * GROUP + j)

    def gather(d):
        t = (j + d) % GROUP
        return remote(glob_piece(j), glob_piece(j), s3s.at[d], s3r.at[d], base + t)

    keep = pltpu.make_async_copy(tok_in.at[pl.ds(0, NG)], tok.at[pl.ds(glob, NG)], loc.at[5])

    @pl.when(me == 0)
    def _():
        for d in range(1, GROUP):
            scatter(d).start()
        keep.start()

    to_left = remote(tok_in.at[pl.ds(0, BLOCK)], tok.at[pl.ds(right_at, BLOCK)], halo_s.at[0], halo_r.at[0], me - 1)
    to_right = remote(
        tok_in.at[pl.ds(rows - BLOCK, BLOCK)], tok.at[pl.ds(0, BLOCK)], halo_s.at[1], halo_r.at[1], me + 1
    )

    @pl.when(has_left)
    def _():
        to_left.start()

    @pl.when(has_right)
    def _():
        to_right.start()

    for copy in local[2:]:
        copy.start()

    @pl.when(me == 0)
    def _():
        tok[0:BLOCK] = jnp.zeros((BLOCK, width), BF16)

    @pl.when(me == n - 1)
    def _():
        tok[right_at : right_at + BLOCK] = jnp.zeros((BLOCK, width), BF16)

    tile = 2 * LANES if width % (2 * LANES) == 0 else LANES

    def project(start, count, w, dst):
        @pl.loop(0, width // tile)
        def _(t):
            cols = pl.ds(pl.multiple_of(t * tile, tile), tile)
            dst[start : start + count, cols] = jnp.dot(
                tok[start : start + count], w[:, cols], preferred_element_type=F32
            ).astype(BF16)

    def project_query(start, count, dst):
        first_half = lax.broadcasted_iota(jnp.int32, (NG, tile), 1) % LANES < BLOCK

        @pl.loop(0, width // tile)
        def _(t):
            cols = pl.ds(pl.multiple_of(t * tile, tile), tile)
            res = jnp.dot(tok[start : start + count], wq[:, cols], preferred_element_type=F32) * scale
            for c in range(count // NG):
                part = res[c * NG : (c + 1) * NG]
                dst[2 * c * NG : (2 * c + 1) * NG, cols] = jnp.where(first_half, part, 0.0).astype(BF16)
                dst[(2 * c + 1) * NG : (2 * c + 2) * NG, cols] = jnp.where(first_half, 0.0, part).astype(BF16)

    local[0].wait()
    local[1].wait()
    project_query(own, rows, q)

    def gather_sends():
        for d in range(1, GROUP):
            @pl.when((g > 0) | ((j + d) % GROUP != 0))
            def _():
                gather(d).start()

    @pl.when(g == 0)
    def _():
        @pl.when(j > 0)
        def _():
            remote(glob_piece(j), glob_piece(j), s1s.at[0], s1r.at[0], 0).wait_recv()

        @pl.when(j == 0)
        def _():
            keep.wait()

        for other in range(1, groups):
            climb(other).start()
        gather_sends()

    local[2].wait()
    project(own, rows, wk, k)

    @pl.when(g > 0)
    def _():
        remote(glob_piece(j), glob_piece(j), s2s.at[0], s2r.at[0], j).wait_recv()
        gather_sends()

    local[3].wait()
    project(own, rows, wv, v)

    shape = (2 * NG, NG + 2 * BLOCK)
    row_block = lax.broadcasted_iota(jnp.int32, shape, 0) % NG // BLOCK
    key_id = lax.broadcasted_iota(jnp.int32, shape, 1)
    apart = key_id // BLOCK - row_block
    for c in range(chunks):
        place = me * rows + (c * NG - BLOCK) + key_id
        ok = (apart >= 0) & (apart <= 2) & (place >= NG) & (place < n * rows)
        mask[c] = jnp.where(ok, 0.0, -jnp.inf).astype(F32)

    @pl.when(has_left)
    def _():
        to_right.wait_recv()

    @pl.when(has_right)
    def _():
        to_left.wait_recv()

    for w, dst in ((wk, k), (wv, v)):
        project(0, BLOCK, w, dst)
        project(right_at, BLOCK, w, dst)

    @pl.when(me > 0)
    def _():
        for d in range(1, GROUP):
            t = (j + GROUP - d) % GROUP
            remote(glob_piece(t), glob_piece(t), s3s.at[d], s3r.at[d], base + t).wait_recv()

    project_query(glob, NG, qg)

    lane = lax.broadcasted_iota(jnp.int32, (NG, LANES), 1)
    low = lane < BLOCK
    def encode(x):
        hi = x.astype(BF16)
        rest = x - hi.astype(F32)
        mid = rest.astype(BF16)
        lo = (rest - mid.astype(F32)).astype(BF16)
        return (
            hi.astype(F32) + pltpu.roll(mid.astype(F32), 16, 1) + pltpu.roll(lo.astype(F32), 32, 1)
        ).astype(BF16)

    def decode(x):
        x = x.astype(F32)
        return x + pltpu.roll(x, LANES - 16, 1) + pltpu.roll(x, LANES - 32, 1)

    def part(index):
        return pl.ds(pl.multiple_of(index * PIECE, PIECE), PIECE)

    hp = pairs // 2
    wide = hp * LANES

    def spread(h, d):
        t = (j + d) % GROUP
        return remote(pacc.at[h, part(t)], racc.at[h, d], r1s.at[h, d], r1r.at[h, d], base + t)

    for h in range(2):
        st = jnp.zeros((NG, LANES), F32)
        for i in range(hp):
            cols = slice((h * hp + i) * LANES, (h * hp + i + 1) * LANES)
            s = dot_t(qg[:, cols], k[own : own + rows, cols])
            top = jnp.max(s, axis=-1, keepdims=True)
            e = jnp.exp(s - top)
            total = jnp.sum(e, axis=-1, keepdims=True)
            o = jnp.dot(e.astype(BF16), v[own : own + rows, cols], preferred_element_type=F32)
            pacc[h, :, i * LANES : (i + 1) * LANES] = jnp.where(low, o[:NG], o[NG:]).astype(BF16)
            st = jnp.where(lane == 2 * i, top[:NG], st)
            st = jnp.where(lane == 2 * i + 1, top[NG:], st)
            st = jnp.where(lane == BLOCK + 2 * i, total[:NG], st)
            st = jnp.where(lane == BLOCK + 2 * i + 1, total[NG:], st)
        pacc[h, :, wide:] = encode(st)
        for d in range(1, GROUP):
            spread(h, d).start()
        racc[h, 0] = pacc[h, part(j)]

    small_lane = lax.broadcasted_iota(jnp.int32, (PIECE, LANES), 1)
    small_low = small_lane < BLOCK

    def per_head(x, p, offset):
        return jnp.where(
            small_low, x[:, offset + 2 * p : offset + 2 * p + 1], x[:, offset + 2 * p + 1 : offset + 2 * p + 2]
        )

    def combine(count, accs, h):
        st = [decode(accs[h, d, :, wide:]) for d in range(count)]
        top = functools.reduce(jnp.maximum, st)
        factors = [jnp.exp(s - top) for s in st]
        total = sum(pltpu.roll(f, BLOCK, 1) * s for f, s in zip(factors, st))
        sums = []
        for p in range(hp):
            cols = slice(p * LANES, (p + 1) * LANES)
            sums.append(sum(per_head(factors[d], p, 0) * accs[h, d, :, cols].astype(F32) for d in range(count)))
        st = jnp.where(small_low, top, total)
        return sums, jnp.where(small_lane % BLOCK < 2 * hp, st, 0.0)

    def window(c, p):
        cols = pl.ds(pl.multiple_of(p * LANES, LANES), LANES)
        span = slice(c * NG, c * NG + NG + 2 * BLOCK)
        qs = q[2 * c * NG : 2 * (c + 1) * NG, cols]
        sw = dot_t(qs, k[span, cols]) + mask[c]
        sg = dot_t(qs, k[glob : glob + NG, cols])
        top = jnp.maximum(jnp.max(sw, axis=-1, keepdims=True), jnp.max(sg, axis=-1, keepdims=True))
        ew = jnp.exp(sw - top)
        eg = jnp.exp(sg - top)
        total = jnp.sum(ew, axis=-1, keepdims=True) + jnp.sum(eg, axis=-1, keepdims=True)
        o = jnp.dot(ew.astype(BF16), v[span, cols], preferred_element_type=F32)
        o = o + jnp.dot(eg.astype(BF16), v[glob : glob + NG, cols], preferred_element_type=F32)
        o = o / total
        att[c * NG : (c + 1) * NG, cols] = jnp.where(low, o[:NG], o[NG:]).astype(BF16)

    def windows(c, first, last):
        @pl.loop(first, last, step=2)
        def _(p):
            window(c, p)
            window(c, p + 1)

    def finish(c):
        at = slice(c * NG, (c + 1) * NG)
        proj = jnp.dot(att[at], wo[...], preferred_element_type=F32)
        summed = tok[own + c * NG : own + (c + 1) * NG].astype(F32) + proj
        center = summed - jnp.mean(summed, axis=-1, keepdims=True)
        spread_ = jnp.mean(center * center, axis=-1, keepdims=True)
        out_ref[at] = (center * lax.rsqrt(spread_ + 1e-05) * gain_ref[...][None] + bias_ref[...][None]).astype(BF16)

    for w, dst in ((wk, k), (wv, v)):
        project(glob, NG, w, dst)

    last = chunks - 1
    early = min(4, pairs)
    windows(last, 0, early)

    def raise_up(h):
        return remote(cacc.at[h], zacc.at[h, g], r2s.at[h], r2r.at[h, g], j)

    for h in range(2):
        for d in range(1, GROUP):
            spread(h, d).wait_recv()
        sums, st = combine(GROUP, racc, h)
        sent = [x.astype(BF16) for x in sums] + [encode(st)]

        @pl.when(g == 0)
        def _():
            for p in range(hp + 1):
                zacc[h, 0, :, p * LANES : (p + 1) * LANES] = sent[p]

        @pl.when(g > 0)
        def _():
            for p in range(hp + 1):
                cacc[h, :, p * LANES : (p + 1) * LANES] = sent[p]
            raise_up(h).start()

    windows(last, early, pairs)
    for c in range(last):
        windows(c, 0, pairs)

    def deliver(h):
        return remote(piece.at[h], gout.at[h, part(j)], r3s.at[h], r3r.at[h, j], 0)

    @pl.when(g == 0)
    def _():
        for h in range(2):
            for other in range(1, groups):
                remote(
                    cacc.at[h], zacc.at[h, other], r2s.at[h], r2r.at[h, other], other * GROUP + j
                ).wait_recv()
            full, full_st = combine(groups, zacc, h)
            for p in range(hp):
                piece[h, :, p * LANES : (p + 1) * LANES] = (full[p] / per_head(full_st, p, BLOCK)).astype(BF16)

            @pl.when(j > 0)
            def _():
                deliver(h).start()

            @pl.when(j == 0)
            def _():
                gout[h, 0:PIECE] = piece[h]

    for copy in local[4:]:
        copy.wait()
    for c in range(1, chunks):
        finish(c)

    @pl.when(me == 0)
    def _():
        for h in range(2):
            for d in range(1, GROUP):
                remote(
                    piece.at[h], gout.at[h, pl.ds(d * PIECE, PIECE)], r3s.at[h], r3r.at[h, d], d
                ).wait_recv()
            att[0:NG, h * wide : (h + 1) * wide] = gout[h]

    finish(0)

    @pl.when(has_left)
    def _():
        to_left.wait_send()

    @pl.when(has_right)
    def _():
        to_right.wait_send()

    @pl.when(me == 0)
    def _():
        for d in range(1, GROUP):
            scatter(d).wait_send()

    @pl.when(g == 0)
    def _():
        for other in range(1, groups):
            climb(other).wait_send()

        @pl.when(j > 0)
        def _():
            for h in range(2):
                deliver(h).wait_send()

    @pl.when(g > 0)
    def _():
        for h in range(2):
            raise_up(h).wait_send()

    for d in range(1, GROUP):
        @pl.when((g > 0) | ((j + d) % GROUP != 0))
        def _():
            gather(d).wait_send()

        for h in range(2):
            spread(h, d).wait_send()


def shards(n, tokens, w_query, w_key, w_value, w_out, ln_gain, ln_bias):
    rows, width = tokens.shape
    groups = n // GROUP
    ext = rows + 2 * BLOCK + NG
    wide = width // 2
    dma = pltpu.SemaphoreType.DMA
    weight = pltpu.VMEM((width, width), BF16)
    scratch = [
        pltpu.VMEM((ext, width), BF16),
        weight, weight, weight, weight,
        pltpu.VMEM((width,), F32),
        pltpu.VMEM((width,), F32),
        pltpu.VMEM((2 * rows, width), BF16),
        pltpu.VMEM((ext, width), BF16),
        pltpu.VMEM((ext, width), BF16),
        pltpu.VMEM((2 * NG, width), BF16),
        pltpu.VMEM((rows // NG, 2 * NG, NG + 2 * BLOCK), F32),
        pltpu.VMEM((2, NG, wide + LANES), BF16),
        pltpu.VMEM((2, GROUP, PIECE, wide + LANES), BF16),
        pltpu.VMEM((2, PIECE, wide + LANES), BF16),
        pltpu.VMEM((2, groups, PIECE, wide + LANES), BF16),
        pltpu.VMEM((2, PIECE, wide), BF16),
        pltpu.VMEM((2, NG, wide), BF16),
        pltpu.VMEM((rows, width), BF16),
        dma((8,)), dma((2,)), dma((2,)),
        dma((GROUP,)), dma((1,)),
        dma((groups,)), dma((1,)),
        dma((GROUP,)), dma((GROUP,)),
        dma((2, GROUP)), dma((2, GROUP)),
        dma((2,)), dma((2, groups)),
        dma((2,)), dma((2, GROUP)),
    ]
    anywhere = pl.BlockSpec(memory_space=pl.ANY)
    vmem = pl.BlockSpec(memory_space=pltpu.VMEM)
    return pl.pallas_call(
        functools.partial(kernel, n),
        out_shape=jax.ShapeDtypeStruct((rows, width), BF16),
        in_specs=[anywhere] * 7,
        out_specs=vmem,
        scratch_shapes=scratch,
        compiler_params=pltpu.CompilerParams(
            collective_id=0, has_side_effects=True, vmem_limit_bytes=60 * 1024 * 1024
        ),
    )(tokens, w_query, w_key, w_value, w_out, ln_gain, ln_bias)


def solution(mesh):
    n = mesh.shape["seq"]
    in_specs = (P("seq", None), P(), P(), P(), P(), P(), P())
    return jax.shard_map(
        functools.partial(shards, n), mesh=mesh, in_specs=in_specs, out_specs=P("seq", None), check_vma=False
    )
```

```python
import functools
import math

import jax
import jax.numpy as jnp
from jax import lax
from jax.experimental import pallas as pl
from jax.experimental.pallas import tpu as pltpu
from jax.sharding import PartitionSpec as P

H = 12
BLOCK = 64
NG = 128
GROUP = 8
PIECE = NG // GROUP
LANES = 128
MESH = pl.DeviceIdType.MESH
BF16 = jnp.bfloat16
F32 = jnp.float32


def dot_t(a, b):
    return lax.dot_general(a, b, (((1,), (1,)), ((), ())), preferred_element_type=F32)


def kernel(
    n, tok_in, wq_in, wk_in, wv_in, wo_in, gain_in, bias_in, out_ref,
    tok, wq, wk, wv, wo, gain_ref, bias_ref, q, k, v, qg, mask, pacc, racc, cacc, zacc,
    piece, gout, att,
    loc, halo_s, halo_r, s1s, s1r, s2s, s2r, s3s, s3r, r1s, r1r, r2s, r2r, r3s, r3r,
):
    rows, width = tok_in.shape
    chunks = rows // NG
    pairs = width // LANES
    groups = n // GROUP
    scale = 1.0 / math.sqrt(width // H)
    own = BLOCK
    left_at = rows
    right_at = rows + BLOCK
    glob = rows + 2 * BLOCK
    me = lax.axis_index("seq")
    g = me // GROUP
    j = me % GROUP
    base = g * GROUP

    def remote(src, dst, ss, rs, dev):
        return pltpu.make_async_remote_copy(
            src_ref=src, dst_ref=dst, send_sem=ss, recv_sem=rs, device_id=(dev,), device_id_type=MESH
        )

    local = [
        pltpu.make_async_copy(tok_in, tok.at[pl.ds(0, rows)], loc.at[0]),
        pltpu.make_async_copy(wq_in, wq, loc.at[1]),
        pltpu.make_async_copy(wk_in, wk, loc.at[2]),
        pltpu.make_async_copy(wv_in, wv, loc.at[3]),
        pltpu.make_async_copy(wo_in, wo, loc.at[4]),
        pltpu.make_async_copy(gain_in, gain_ref, loc.at[6]),
        pltpu.make_async_copy(bias_in, bias_ref, loc.at[7]),
    ]
    for copy in local[:2]:
        copy.start()

    barrier = pltpu.get_barrier_semaphore()

    def greet(dev):
        pl.semaphore_signal(barrier, inc=1, device_id=(dev,), device_id_type=MESH)

    for d in range(1, GROUP):
        greet(base + (j + d) % GROUP)

    @pl.when(g == 0)
    def _():
        for other in range(1, groups):
            greet(other * GROUP + j)

    @pl.when(g > 0)
    def _():
        greet(j)

    has_left = me > 0
    has_right = me < n - 1
    cross_left = (j == 0) & (g > 0)
    cross_right = (j == GROUP - 1) & (g < groups - 1)

    @pl.when(cross_left)
    def _():
        greet(me - 1)

    @pl.when(cross_right)
    def _():
        greet(me + 1)

    peers = GROUP - 1 + jnp.where(g == 0, groups - 1, 1) + jnp.where(cross_left, 1, 0) + jnp.where(cross_right, 1, 0)
    pl.semaphore_wait(barrier, peers)

    def glob_piece(index):
        return tok.at[pl.ds(pl.multiple_of(glob + index * PIECE, PIECE), PIECE)]

    def scatter(d):
        return remote(tok_in.at[pl.ds(d * PIECE, PIECE)], glob_piece(d), s1s.at[d], s1r.at[0], d)

    def climb(other):
        return remote(glob_piece(j), glob_piece(j), s2s.at[other], s2r.at[0], other * GROUP + j)

    def gather(d):
        t = (j + d) % GROUP
        return remote(glob_piece(j), glob_piece(j), s3s.at[d], s3r.at[d], base + t)

    keep = pltpu.make_async_copy(tok_in.at[pl.ds(0, NG)], tok.at[pl.ds(glob, NG)], loc.at[5])

    @pl.when(me == 0)
    def _():
        for d in range(1, GROUP):
            scatter(d).start()
        keep.start()

    to_left = remote(tok_in.at[pl.ds(0, BLOCK)], tok.at[pl.ds(right_at, BLOCK)], halo_s.at[0], halo_r.at[0], me - 1)
    to_right = remote(
        tok_in.at[pl.ds(rows - BLOCK, BLOCK)], tok.at[pl.ds(left_at, BLOCK)], halo_s.at[1], halo_r.at[1], me + 1
    )

    @pl.when(has_left)
    def _():
        to_left.start()

    @pl.when(has_right)
    def _():
        to_right.start()

    for copy in local[2:]:
        copy.start()

    @pl.when(me == 0)
    def _():
        tok[left_at : left_at + BLOCK] = jnp.zeros((BLOCK, width), BF16)

    @pl.when(me == n - 1)
    def _():
        tok[right_at : right_at + BLOCK] = jnp.zeros((BLOCK, width), BF16)

    tile = 2 * LANES if width % (2 * LANES) == 0 else LANES

    def project(w, dst, pieces):
        start, count = pieces[0][0], sum(piece_[2] for piece_ in pieces)
        for t in range(width // tile):
            cols = slice(t * tile, (t + 1) * tile)
            res = jnp.dot(tok[start : start + count], w[:, cols], preferred_element_type=F32).astype(BF16)
            for src, to, size in pieces:
                dst[to : to + size, cols] = res[src - start : src - start + size]

    def project_query(start, count, dst):
        first_half = lax.broadcasted_iota(jnp.int32, (NG, tile), 1) % LANES < BLOCK

        for t in range(width // tile):
            cols = slice(t * tile, (t + 1) * tile)
            res = jnp.dot(tok[start : start + count], wq[:, cols], preferred_element_type=F32) * scale
            for c in range(count // NG):
                part = res[c * NG : (c + 1) * NG]
                dst[2 * c * NG : (2 * c + 1) * NG, cols] = jnp.where(first_half, part, 0.0).astype(BF16)
                dst[(2 * c + 1) * NG : (2 * c + 2) * NG, cols] = jnp.where(first_half, 0.0, part).astype(BF16)

    local[0].wait()
    local[1].wait()
    project_query(0, rows, q)

    def gather_sends():
        for d in range(1, GROUP):
            @pl.when((g > 0) | ((j + d) % GROUP != 0))
            def _():
                gather(d).start()

    @pl.when(g == 0)
    def _():
        @pl.when(j > 0)
        def _():
            remote(glob_piece(j), glob_piece(j), s1s.at[0], s1r.at[0], 0).wait_recv()

        @pl.when(j == 0)
        def _():
            keep.wait()

        for other in range(1, groups):
            climb(other).start()
        gather_sends()

    local[2].wait()
    project(wk, k, [(0, own, rows)])

    @pl.when(g > 0)
    def _():
        remote(glob_piece(j), glob_piece(j), s2s.at[0], s2r.at[0], j).wait_recv()
        gather_sends()

    local[3].wait()
    project(wv, v, [(0, own, rows)])

    shape = (2 * NG, NG + 2 * BLOCK)
    row_block = lax.broadcasted_iota(jnp.int32, shape, 0) % NG // BLOCK
    key_id = lax.broadcasted_iota(jnp.int32, shape, 1)
    apart = key_id // BLOCK - row_block
    for c in range(chunks):
        place = me * rows + (c * NG - BLOCK) + key_id
        ok = (apart >= 0) & (apart <= 2) & (place >= NG) & (place < n * rows)
        mask[c] = jnp.where(ok, 0.0, -jnp.inf).astype(F32)

    @pl.when(me > 0)
    def _():
        for d in range(1, GROUP):
            t = (j + GROUP - d) % GROUP
            remote(glob_piece(t), glob_piece(t), s3s.at[d], s3r.at[d], base + t).wait_recv()

    project_query(glob, NG, qg)

    lane = lax.broadcasted_iota(jnp.int32, (NG, LANES), 1)
    low = lane < BLOCK
    def encode(x):
        hi = x.astype(BF16)
        rest = x - hi.astype(F32)
        mid = rest.astype(BF16)
        lo = (rest - mid.astype(F32)).astype(BF16)
        return (
            hi.astype(F32) + pltpu.roll(mid.astype(F32), 16, 1) + pltpu.roll(lo.astype(F32), 32, 1)
        ).astype(BF16)

    def decode(x):
        x = x.astype(F32)
        return x + pltpu.roll(x, LANES - 16, 1) + pltpu.roll(x, LANES - 32, 1)

    def part(index):
        return pl.ds(pl.multiple_of(index * PIECE, PIECE), PIECE)

    hp = pairs // 2
    wide = hp * LANES

    def spread(h, d):
        t = (j + d) % GROUP
        return remote(pacc.at[h, part(t)], racc.at[h, d], r1s.at[h, d], r1r.at[h, d], base + t)

    for h in range(2):
        st = jnp.zeros((NG, LANES), F32)
        for i in range(hp):
            cols = slice((h * hp + i) * LANES, (h * hp + i + 1) * LANES)
            s = dot_t(qg[:, cols], k[own : own + rows, cols])
            top = jnp.max(s, axis=-1, keepdims=True)
            e = jnp.exp(s - top)
            total = jnp.sum(e, axis=-1, keepdims=True)
            o = jnp.dot(e.astype(BF16), v[own : own + rows, cols], preferred_element_type=F32)
            pacc[h, :, i * LANES : (i + 1) * LANES] = jnp.where(low, o[:NG], o[NG:]).astype(BF16)
            st = jnp.where(lane == 2 * i, top[:NG], st)
            st = jnp.where(lane == 2 * i + 1, top[NG:], st)
            st = jnp.where(lane == BLOCK + 2 * i, total[:NG], st)
            st = jnp.where(lane == BLOCK + 2 * i + 1, total[NG:], st)
        pacc[h, :, wide:] = encode(st)
        for d in range(1, GROUP):
            spread(h, d).start()
        racc[h, 0] = pacc[h, part(j)]

    small_lane = lax.broadcasted_iota(jnp.int32, (PIECE, LANES), 1)
    small_low = small_lane < BLOCK

    def per_head(x, p, offset):
        return jnp.where(
            small_low, x[:, offset + 2 * p : offset + 2 * p + 1], x[:, offset + 2 * p + 1 : offset + 2 * p + 2]
        )

    def combine(count, accs, h):
        st = [decode(accs[h, d, :, wide:]) for d in range(count)]
        top = functools.reduce(jnp.maximum, st)
        factors = [jnp.exp(s - top) for s in st]
        total = sum(pltpu.roll(f, BLOCK, 1) * s for f, s in zip(factors, st))
        sums = []
        for p in range(hp):
            cols = slice(p * LANES, (p + 1) * LANES)
            sums.append(sum(per_head(factors[d], p, 0) * accs[h, d, :, cols].astype(F32) for d in range(count)))
        st = jnp.where(small_low, top, total)
        return sums, jnp.where(small_lane % BLOCK < 2 * hp, st, 0.0)

    def window(c, p):
        cols = pl.ds(pl.multiple_of(p * LANES, LANES), LANES)
        span = slice(c * NG, c * NG + NG + 2 * BLOCK)
        qs = q[2 * c * NG : 2 * (c + 1) * NG, cols]
        sw = dot_t(qs, k[span, cols]) + mask[c]
        sg = dot_t(qs, k[glob : glob + NG, cols])
        top = jnp.maximum(jnp.max(sw, axis=-1, keepdims=True), jnp.max(sg, axis=-1, keepdims=True))
        ew = jnp.exp(sw - top)
        eg = jnp.exp(sg - top)
        total = jnp.sum(ew, axis=-1, keepdims=True) + jnp.sum(eg, axis=-1, keepdims=True)
        o = jnp.dot(ew.astype(BF16), v[span, cols], preferred_element_type=F32)
        o = o + jnp.dot(eg.astype(BF16), v[glob : glob + NG, cols], preferred_element_type=F32)
        o = o / total
        att[c * NG : (c + 1) * NG, cols] = jnp.where(low, o[:NG], o[NG:]).astype(BF16)

    def windows(c, first, last):
        @pl.loop(first, last, step=2)
        def _(p):
            window(c, p)
            window(c, p + 1)

    def finish(c):
        at = slice(c * NG, (c + 1) * NG)
        proj = jnp.dot(att[at], wo[...], preferred_element_type=F32)
        summed = tok[c * NG : (c + 1) * NG].astype(F32) + proj
        center = summed - jnp.mean(summed, axis=-1, keepdims=True)
        spread_ = jnp.mean(center * center, axis=-1, keepdims=True)
        out_ref[at] = (center * lax.rsqrt(spread_ + 1e-05) * gain_ref[...][None] + bias_ref[...][None]).astype(BF16)

    @pl.when(has_left)
    def _():
        to_right.wait_recv()

    @pl.when(has_right)
    def _():
        to_left.wait_recv()

    for w, dst in ((wk, k), (wv, v)):
        project(w, dst, [(left_at, 0, BLOCK), (right_at, own + rows, BLOCK), (glob, glob, NG)])

    last = chunks - 1
    early = min(2, pairs)
    windows(last, 0, early)

    def raise_up(h):
        return remote(cacc.at[h], zacc.at[h, g], r2s.at[h], r2r.at[h, g], j)

    for h in range(2):
        for d in range(1, GROUP):
            spread(h, d).wait_recv()
        sums, st = combine(GROUP, racc, h)
        sent = [x.astype(BF16) for x in sums] + [encode(st)]

        @pl.when(g == 0)
        def _():
            for p in range(hp + 1):
                zacc[h, 0, :, p * LANES : (p + 1) * LANES] = sent[p]

        @pl.when(g > 0)
        def _():
            for p in range(hp + 1):
                cacc[h, :, p * LANES : (p + 1) * LANES] = sent[p]
            raise_up(h).start()

    windows(last, early, pairs)
    for c in range(last):
        windows(c, 0, pairs)

    def deliver(h):
        return remote(piece.at[h], gout.at[h, part(j)], r3s.at[h], r3r.at[h, j], 0)

    @pl.when(g == 0)
    def _():
        for h in range(2):
            for other in range(1, groups):
                remote(
                    cacc.at[h], zacc.at[h, other], r2s.at[h], r2r.at[h, other], other * GROUP + j
                ).wait_recv()
            full, full_st = combine(groups, zacc, h)
            for p in range(hp):
                piece[h, :, p * LANES : (p + 1) * LANES] = (full[p] / per_head(full_st, p, BLOCK)).astype(BF16)

            @pl.when(j > 0)
            def _():
                deliver(h).start()

            @pl.when(j == 0)
            def _():
                gout[h, 0:PIECE] = piece[h]

    for copy in local[4:]:
        copy.wait()
    for c in range(1, chunks):
        finish(c)

    @pl.when(me == 0)
    def _():
        for h in range(2):
            for d in range(1, GROUP):
                remote(
                    piece.at[h], gout.at[h, pl.ds(d * PIECE, PIECE)], r3s.at[h], r3r.at[h, d], d
                ).wait_recv()
            att[0:NG, h * wide : (h + 1) * wide] = gout[h]

    finish(0)

    @pl.when(has_left)
    def _():
        to_left.wait_send()

    @pl.when(has_right)
    def _():
        to_right.wait_send()

    @pl.when(me == 0)
    def _():
        for d in range(1, GROUP):
            scatter(d).wait_send()

    @pl.when(g == 0)
    def _():
        for other in range(1, groups):
            climb(other).wait_send()

        @pl.when(j > 0)
        def _():
            for h in range(2):
                deliver(h).wait_send()

    @pl.when(g > 0)
    def _():
        for h in range(2):
            raise_up(h).wait_send()

    for d in range(1, GROUP):
        @pl.when((g > 0) | ((j + d) % GROUP != 0))
        def _():
            gather(d).wait_send()

        for h in range(2):
            spread(h, d).wait_send()


def shards(n, tokens, w_query, w_key, w_value, w_out, ln_gain, ln_bias):
    rows, width = tokens.shape
    groups = n // GROUP
    ext = rows + 2 * BLOCK + NG
    wide = width // 2
    dma = pltpu.SemaphoreType.DMA
    weight = pltpu.VMEM((width, width), BF16)
    scratch = [
        pltpu.VMEM((ext, width), BF16),
        weight, weight, weight, weight,
        pltpu.VMEM((width,), F32),
        pltpu.VMEM((width,), F32),
        pltpu.VMEM((2 * rows, width), BF16),
        pltpu.VMEM((ext, width), BF16),
        pltpu.VMEM((ext, width), BF16),
        pltpu.VMEM((2 * NG, width), BF16),
        pltpu.VMEM((rows // NG, 2 * NG, NG + 2 * BLOCK), F32),
        pltpu.VMEM((2, NG, wide + LANES), BF16),
        pltpu.VMEM((2, GROUP, PIECE, wide + LANES), BF16),
        pltpu.VMEM((2, PIECE, wide + LANES), BF16),
        pltpu.VMEM((2, groups, PIECE, wide + LANES), BF16),
        pltpu.VMEM((2, PIECE, wide), BF16),
        pltpu.VMEM((2, NG, wide), BF16),
        pltpu.VMEM((rows, width), BF16),
        dma((8,)), dma((2,)), dma((2,)),
        dma((GROUP,)), dma((1,)),
        dma((groups,)), dma((1,)),
        dma((GROUP,)), dma((GROUP,)),
        dma((2, GROUP)), dma((2, GROUP)),
        dma((2,)), dma((2, groups)),
        dma((2,)), dma((2, GROUP)),
    ]
    anywhere = pl.BlockSpec(memory_space=pl.ANY)
    vmem = pl.BlockSpec(memory_space=pltpu.VMEM)
    return pl.pallas_call(
        functools.partial(kernel, n),
        out_shape=jax.ShapeDtypeStruct((rows, width), BF16),
        in_specs=[anywhere] * 7,
        out_specs=vmem,
        scratch_shapes=scratch,
        compiler_params=pltpu.CompilerParams(
            collective_id=0, has_side_effects=True, vmem_limit_bytes=60 * 1024 * 1024
        ),
    )(tokens, w_query, w_key, w_value, w_out, ln_gain, ln_bias)


def solution(mesh):
    n = mesh.shape["seq"]
    in_specs = (P("seq", None), P(), P(), P(), P(), P(), P())
    return jax.shard_map(
        functools.partial(shards, n), mesh=mesh, in_specs=in_specs, out_specs=P("seq", None), check_vma=False
    )
```

```python
import functools
import math

import jax
import jax.numpy as jnp
from jax import lax
from jax.experimental import pallas as pl
from jax.experimental.pallas import tpu as pltpu
from jax.sharding import PartitionSpec as P

H = 12
BLOCK = 64
NG = 128
GROUP = 8
PIECE = NG // GROUP
LANES = 128
MESH = pl.DeviceIdType.MESH
BF16 = jnp.bfloat16
F32 = jnp.float32


def dot_t(a, b):
    return lax.dot_general(a, b, (((1,), (1,)), ((), ())), preferred_element_type=F32)


def kernel(
    n, tok_in, wq_in, wk_in, wv_in, wo_in, gain_in, bias_in, out_ref,
    tok, wq, wk, wv, wo, gain_ref, bias_ref, q, k, v, qg, mask, pacc, racc, cacc, zacc,
    piece, gout, att,
    loc, halo_s, halo_r, s1s, s1r, s2s, s2x, s2r, s3s, s3r, r1s, r1r, r2s, r2r, r3s, r3r,
):
    rows, width = tok_in.shape
    chunks = rows // NG
    pairs = width // LANES
    groups = n // GROUP
    scale = 1.0 / math.sqrt(width // H)
    own = BLOCK
    left_at = rows
    right_at = rows + BLOCK
    glob = rows + 2 * BLOCK
    me = lax.axis_index("seq")
    g = me // GROUP
    j = me % GROUP
    base = g * GROUP

    def remote(src, dst, ss, rs, dev):
        return pltpu.make_async_remote_copy(
            src_ref=src, dst_ref=dst, send_sem=ss, recv_sem=rs, device_id=(dev,), device_id_type=MESH
        )

    local = [
        pltpu.make_async_copy(tok_in, tok.at[pl.ds(0, rows)], loc.at[0]),
        pltpu.make_async_copy(wq_in, wq, loc.at[1]),
        pltpu.make_async_copy(wk_in, wk, loc.at[2]),
        pltpu.make_async_copy(wv_in, wv, loc.at[3]),
        pltpu.make_async_copy(wo_in, wo, loc.at[4]),
        pltpu.make_async_copy(gain_in, gain_ref, loc.at[6]),
        pltpu.make_async_copy(bias_in, bias_ref, loc.at[7]),
    ]
    for copy in local[:2]:
        copy.start()

    barrier = pltpu.get_barrier_semaphore()

    def greet(dev):
        pl.semaphore_signal(barrier, inc=1, device_id=(dev,), device_id_type=MESH)

    for d in range(1, GROUP):
        greet(base + (j + d) % GROUP)

    @pl.when(g == 0)
    def _():
        for other in range(1, groups):
            greet(other * GROUP + j)

    @pl.when(g > 0)
    def _():
        greet(jnp.where(j == 0, 1, j))

    has_left = me > 0
    has_right = me < n - 1
    cross_left = (j == 0) & (g > 0)
    cross_right = (j == GROUP - 1) & (g < groups - 1)

    @pl.when(cross_left)
    def _():
        greet(me - 1)

    @pl.when(cross_right)
    def _():
        greet(me + 1)

    column = jnp.where(j == 0, 0, groups - 1) + jnp.where(j == 1, groups - 1, 0)
    peers = GROUP - 1 + jnp.where(g == 0, column, 1) + jnp.where(cross_left, 1, 0) + jnp.where(cross_right, 1, 0)
    pl.semaphore_wait(barrier, peers)

    def glob_piece(index):
        return tok.at[pl.ds(pl.multiple_of(glob + index * PIECE, PIECE), PIECE)]

    wide = pairs // 2 * LANES

    def scatter(d):
        first, count = (0, 2 * PIECE) if d == 1 else (d * PIECE, PIECE)
        return remote(
            tok_in.at[pl.ds(first, count)], tok.at[pl.ds(glob + first, count)], s1s.at[d], s1r.at[0], d
        )

    def glob_half(index, h):
        return tok.at[pl.ds(pl.multiple_of(glob + index * PIECE, PIECE), PIECE), pl.ds(h * wide, wide)]

    def climb(other, h):
        return remote(glob_half(j, h), glob_half(j, h), s2s.at[h, other], s2r.at[h], other * GROUP + j)

    def climb_first(other, h):
        return remote(glob_half(0, h), glob_half(0, h), s2x.at[h, other], s2r.at[h], other * GROUP)

    def gather(h, d):
        t = (j + d) % GROUP
        return remote(glob_half(j, h), glob_half(j, h), s3s.at[h, d], s3r.at[h, d], base + t)

    def gathers(d):
        wanted = (j + d) % GROUP != 0
        if d == 1:
            wanted = wanted & (j > 0)
        return (g > 0) | wanted

    keep = pltpu.make_async_copy(tok_in.at[pl.ds(0, NG)], tok.at[pl.ds(glob, NG)], loc.at[5])

    @pl.when(me == 0)
    def _():
        for d in range(1, GROUP):
            scatter(d).start()
        keep.start()

    to_left = remote(tok_in.at[pl.ds(0, BLOCK)], tok.at[pl.ds(right_at, BLOCK)], halo_s.at[0], halo_r.at[0], me - 1)
    to_right = remote(
        tok_in.at[pl.ds(rows - BLOCK, BLOCK)], tok.at[pl.ds(left_at, BLOCK)], halo_s.at[1], halo_r.at[1], me + 1
    )

    @pl.when(has_left)
    def _():
        to_left.start()

    @pl.when(has_right)
    def _():
        to_right.start()

    for copy in local[2:]:
        copy.start()

    @pl.when(me == 0)
    def _():
        tok[left_at : left_at + BLOCK] = jnp.zeros((BLOCK, width), BF16)

    @pl.when(me == n - 1)
    def _():
        tok[right_at : right_at + BLOCK] = jnp.zeros((BLOCK, width), BF16)

    tile = 2 * LANES if width % (2 * LANES) == 0 else LANES

    def project(w, dst, pieces):
        start, count = pieces[0][0], sum(piece_[2] for piece_ in pieces)
        for t in range(width // tile):
            cols = slice(t * tile, (t + 1) * tile)
            res = jnp.dot(tok[start : start + count], w[:, cols], preferred_element_type=F32).astype(BF16)
            for src, to, size in pieces:
                dst[to : to + size, cols] = res[src - start : src - start + size]

    def project_query(start, count, dst):
        first_half = lax.broadcasted_iota(jnp.int32, (NG, tile), 1) % LANES < BLOCK

        for t in range(width // tile):
            cols = slice(t * tile, (t + 1) * tile)
            res = jnp.dot(tok[start : start + count], wq[:, cols], preferred_element_type=F32) * scale
            for c in range(count // NG):
                part = res[c * NG : (c + 1) * NG]
                dst[2 * c * NG : (2 * c + 1) * NG, cols] = jnp.where(first_half, part, 0.0).astype(BF16)
                dst[(2 * c + 1) * NG : (2 * c + 2) * NG, cols] = jnp.where(first_half, 0.0, part).astype(BF16)

    local[0].wait()
    local[1].wait()
    project_query(0, rows, q)

    def gather_sends(h):
        for d in range(1, GROUP):
            @pl.when(gathers(d))
            def _():
                gather(h, d).start()

    @pl.when(g == 0)
    def _():
        @pl.when(j > 1)
        def _():
            remote(glob_piece(j), glob_piece(j), s1s.at[0], s1r.at[0], 0).wait_recv()

        @pl.when(j == 1)
        def _():
            two = tok.at[pl.ds(glob, 2 * PIECE)]
            remote(two, two, s1s.at[0], s1r.at[0], 0).wait_recv()

        @pl.when(j == 0)
        def _():
            keep.wait()

        for h in range(2):
            @pl.when(j > 0)
            def _():
                for other in range(1, groups):
                    climb(other, h).start()

            @pl.when(j == 1)
            def _():
                for other in range(1, groups):
                    climb_first(other, h).start()

        for h in range(2):
            gather_sends(h)

    local[2].wait()
    project(wk, k, [(0, own, rows)])

    @pl.when(g > 0)
    def _():
        for h in range(2):
            remote(glob_half(j, h), glob_half(j, h), s2s.at[h, 0], s2r.at[h], jnp.where(j == 0, 1, j)).wait_recv()
            gather_sends(h)

    local[3].wait()
    project(wv, v, [(0, own, rows)])

    shape = (2 * NG, NG + 2 * BLOCK)
    row_block = lax.broadcasted_iota(jnp.int32, shape, 0) % NG // BLOCK
    key_id = lax.broadcasted_iota(jnp.int32, shape, 1)
    apart = key_id // BLOCK - row_block
    for c in range(chunks):
        place = me * rows + (c * NG - BLOCK) + key_id
        ok = (apart >= 0) & (apart <= 2) & (place >= NG) & (place < n * rows)
        mask[c] = jnp.where(ok, 0.0, -jnp.inf).astype(F32)

    for d in range(1, GROUP):
        @pl.when(me > (1 if d == 1 else 0))
        def _():
            t = (j + GROUP - d) % GROUP
            for h in range(2):
                remote(glob_half(t, h), glob_half(t, h), s3s.at[h, d], s3r.at[h, d], base + t).wait_recv()

    project_query(glob, NG, qg)

    lane = lax.broadcasted_iota(jnp.int32, (NG, LANES), 1)
    low = lane < BLOCK
    def encode(x):
        hi = x.astype(BF16)
        rest = x - hi.astype(F32)
        mid = rest.astype(BF16)
        lo = (rest - mid.astype(F32)).astype(BF16)
        return (
            hi.astype(F32) + pltpu.roll(mid.astype(F32), 16, 1) + pltpu.roll(lo.astype(F32), 32, 1)
        ).astype(BF16)

    def decode(x):
        x = x.astype(F32)
        return x + pltpu.roll(x, LANES - 16, 1) + pltpu.roll(x, LANES - 32, 1)

    def part(index):
        return pl.ds(pl.multiple_of(index * PIECE, PIECE), PIECE)

    hp = pairs // 2

    def spread(h, d):
        t = (j + d) % GROUP
        return remote(pacc.at[h, part(t)], racc.at[h, d], r1s.at[h, d], r1r.at[h, d], base + t)

    for h in range(2):
        st = jnp.zeros((NG, LANES), F32)
        for i in range(hp):
            cols = slice((h * hp + i) * LANES, (h * hp + i + 1) * LANES)
            s = dot_t(qg[:, cols], k[own : own + rows, cols])
            top = jnp.max(s, axis=-1, keepdims=True)
            e = jnp.exp(s - top)
            total = jnp.sum(e, axis=-1, keepdims=True)
            o = jnp.dot(e.astype(BF16), v[own : own + rows, cols], preferred_element_type=F32)
            pacc[h, :, i * LANES : (i + 1) * LANES] = jnp.where(low, o[:NG], o[NG:]).astype(BF16)
            st = jnp.where(lane == 2 * i, top[:NG], st)
            st = jnp.where(lane == 2 * i + 1, top[NG:], st)
            st = jnp.where(lane == BLOCK + 2 * i, total[:NG], st)
            st = jnp.where(lane == BLOCK + 2 * i + 1, total[NG:], st)
        pacc[h, :, wide:] = encode(st)
        for d in range(1, GROUP):
            spread(h, d).start()
        racc[h, 0] = pacc[h, part(j)]

    small_lane = lax.broadcasted_iota(jnp.int32, (PIECE, LANES), 1)
    small_low = small_lane < BLOCK

    def per_head(x, p, offset):
        return jnp.where(
            small_low, x[:, offset + 2 * p : offset + 2 * p + 1], x[:, offset + 2 * p + 1 : offset + 2 * p + 2]
        )

    def combine(count, accs, h):
        st = [decode(accs[h, d, :, wide:]) for d in range(count)]
        top = functools.reduce(jnp.maximum, st)
        factors = [jnp.exp(s - top) for s in st]
        total = sum(pltpu.roll(f, BLOCK, 1) * s for f, s in zip(factors, st))
        sums = []
        for p in range(hp):
            cols = slice(p * LANES, (p + 1) * LANES)
            sums.append(sum(per_head(factors[d], p, 0) * accs[h, d, :, cols].astype(F32) for d in range(count)))
        st = jnp.where(small_low, top, total)
        return sums, jnp.where(small_lane % BLOCK < 2 * hp, st, 0.0)

    def window(c, p):
        cols = pl.ds(pl.multiple_of(p * LANES, LANES), LANES)
        span = slice(c * NG, c * NG + NG + 2 * BLOCK)
        qs = q[2 * c * NG : 2 * (c + 1) * NG, cols]
        sw = dot_t(qs, k[span, cols]) + mask[c]
        sg = dot_t(qs, k[glob : glob + NG, cols])
        top = jnp.maximum(jnp.max(sw, axis=-1, keepdims=True), jnp.max(sg, axis=-1, keepdims=True))
        ew = jnp.exp(sw - top)
        eg = jnp.exp(sg - top)
        total = jnp.sum(ew, axis=-1, keepdims=True) + jnp.sum(eg, axis=-1, keepdims=True)
        o = jnp.dot(ew.astype(BF16), v[span, cols], preferred_element_type=F32)
        o = o + jnp.dot(eg.astype(BF16), v[glob : glob + NG, cols], preferred_element_type=F32)
        o = o / total
        att[c * NG : (c + 1) * NG, cols] = jnp.where(low, o[:NG], o[NG:]).astype(BF16)

    def windows(c, first, last):
        @pl.loop(first, last, step=2)
        def _(p):
            window(c, p)
            window(c, p + 1)

    def finish(c):
        at = slice(c * NG, (c + 1) * NG)
        proj = jnp.dot(att[at], wo[...], preferred_element_type=F32)
        summed = tok[c * NG : (c + 1) * NG].astype(F32) + proj
        center = summed - jnp.mean(summed, axis=-1, keepdims=True)
        spread_ = jnp.mean(center * center, axis=-1, keepdims=True)
        out_ref[at] = (center * lax.rsqrt(spread_ + 1e-05) * gain_ref[...][None] + bias_ref[...][None]).astype(BF16)

    @pl.when(has_left)
    def _():
        to_right.wait_recv()

    @pl.when(has_right)
    def _():
        to_left.wait_recv()

    for w, dst in ((wk, k), (wv, v)):
        project(w, dst, [(left_at, 0, BLOCK), (right_at, own + rows, BLOCK), (glob, glob, NG)])

    last = chunks - 1
    early = min(2, pairs)
    windows(last, 0, early)

    def raise_up(h):
        return remote(cacc.at[h], zacc.at[h, g], r2s.at[h], r2r.at[h, g], j)

    for h in range(2):
        for d in range(1, GROUP):
            spread(h, d).wait_recv()
        sums, st = combine(GROUP, racc, h)
        sent = [x.astype(BF16) for x in sums] + [encode(st)]

        @pl.when(g == 0)
        def _():
            for p in range(hp + 1):
                zacc[h, 0, :, p * LANES : (p + 1) * LANES] = sent[p]

        @pl.when(g > 0)
        def _():
            for p in range(hp + 1):
                cacc[h, :, p * LANES : (p + 1) * LANES] = sent[p]
            raise_up(h).start()

    windows(last, early, pairs)
    for c in range(last):
        windows(c, 0, pairs)

    def deliver(h):
        return remote(piece.at[h], gout.at[h, part(j)], r3s.at[h], r3r.at[h, j], 0)

    @pl.when(g == 0)
    def _():
        for h in range(2):
            for other in range(1, groups):
                remote(
                    cacc.at[h], zacc.at[h, other], r2s.at[h], r2r.at[h, other], other * GROUP + j
                ).wait_recv()
            full, full_st = combine(groups, zacc, h)
            for p in range(hp):
                piece[h, :, p * LANES : (p + 1) * LANES] = (full[p] / per_head(full_st, p, BLOCK)).astype(BF16)

            @pl.when(j > 0)
            def _():
                deliver(h).start()

            @pl.when(j == 0)
            def _():
                gout[h, 0:PIECE] = piece[h]

    for copy in local[4:]:
        copy.wait()
    for c in range(1, chunks):
        finish(c)

    @pl.when(me == 0)
    def _():
        for h in range(2):
            for d in range(1, GROUP):
                remote(
                    piece.at[h], gout.at[h, pl.ds(d * PIECE, PIECE)], r3s.at[h], r3r.at[h, d], d
                ).wait_recv()
            att[0:NG, h * wide : (h + 1) * wide] = gout[h]

    finish(0)

    @pl.when(has_left)
    def _():
        to_left.wait_send()

    @pl.when(has_right)
    def _():
        to_right.wait_send()

    @pl.when(me == 0)
    def _():
        for d in range(1, GROUP):
            scatter(d).wait_send()

    @pl.when(g == 0)
    def _():
        @pl.when(j > 0)
        def _():
            for h in range(2):
                for other in range(1, groups):
                    climb(other, h).wait_send()
                deliver(h).wait_send()

        @pl.when(j == 1)
        def _():
            for h in range(2):
                for other in range(1, groups):
                    climb_first(other, h).wait_send()

    @pl.when(g > 0)
    def _():
        for h in range(2):
            raise_up(h).wait_send()

    for d in range(1, GROUP):
        @pl.when(gathers(d))
        def _():
            for h in range(2):
                gather(h, d).wait_send()

        for h in range(2):
            spread(h, d).wait_send()


def shards(n, tokens, w_query, w_key, w_value, w_out, ln_gain, ln_bias):
    rows, width = tokens.shape
    groups = n // GROUP
    ext = rows + 2 * BLOCK + NG
    wide = width // 2
    dma = pltpu.SemaphoreType.DMA
    weight = pltpu.VMEM((width, width), BF16)
    scratch = [
        pltpu.VMEM((ext, width), BF16),
        weight, weight, weight, weight,
        pltpu.VMEM((width,), F32),
        pltpu.VMEM((width,), F32),
        pltpu.VMEM((2 * rows, width), BF16),
        pltpu.VMEM((ext, width), BF16),
        pltpu.VMEM((ext, width), BF16),
        pltpu.VMEM((2 * NG, width), BF16),
        pltpu.VMEM((rows // NG, 2 * NG, NG + 2 * BLOCK), F32),
        pltpu.VMEM((2, NG, wide + LANES), BF16),
        pltpu.VMEM((2, GROUP, PIECE, wide + LANES), BF16),
        pltpu.VMEM((2, PIECE, wide + LANES), BF16),
        pltpu.VMEM((2, groups, PIECE, wide + LANES), BF16),
        pltpu.VMEM((2, PIECE, wide), BF16),
        pltpu.VMEM((2, NG, wide), BF16),
        pltpu.VMEM((rows, width), BF16),
        dma((8,)), dma((2,)), dma((2,)),
        dma((GROUP,)), dma((1,)),
        dma((2, groups)), dma((2, groups)), dma((2,)),
        dma((2, GROUP)), dma((2, GROUP)),
        dma((2, GROUP)), dma((2, GROUP)),
        dma((2,)), dma((2, groups)),
        dma((2,)), dma((2, GROUP)),
    ]
    anywhere = pl.BlockSpec(memory_space=pl.ANY)
    vmem = pl.BlockSpec(memory_space=pltpu.VMEM)
    return pl.pallas_call(
        functools.partial(kernel, n),
        out_shape=jax.ShapeDtypeStruct((rows, width), BF16),
        in_specs=[anywhere] * 7,
        out_specs=vmem,
        scratch_shapes=scratch,
        compiler_params=pltpu.CompilerParams(
            collective_id=0, has_side_effects=True, vmem_limit_bytes=60 * 1024 * 1024
        ),
    )(tokens, w_query, w_key, w_value, w_out, ln_gain, ln_bias)


def solution(mesh):
    n = mesh.shape["seq"]
    in_specs = (P("seq", None), P(), P(), P(), P(), P(), P())
    return jax.shard_map(
        functools.partial(shards, n), mesh=mesh, in_specs=in_specs, out_specs=P("seq", None), check_vma=False
    )
```

```python
import functools
import math

import jax
import jax.numpy as jnp
from jax import lax
from jax.experimental import pallas as pl
from jax.experimental.pallas import tpu as pltpu
from jax.sharding import PartitionSpec as P

H = 12
BLOCK = 64
NG = 128
GROUP = 8
PIECE = NG // GROUP
LANES = 128
MESH = pl.DeviceIdType.MESH
BF16 = jnp.bfloat16
F32 = jnp.float32


def dot_t(a, b):
    return lax.dot_general(a, b, (((1,), (1,)), ((), ())), preferred_element_type=F32)


def kernel(
    n, tok_in, wq_in, wk_in, wv_in, wo_in, gain_in, bias_in, out_ref,
    tok, wq, wk, wv, wo, gain_ref, bias_ref, q, k, v, qg, mask, pacc, racc, cacc, zacc,
    piece, gout, att,
    loc, halo_s, halo_r, s1s, s1r, s2s, s2x, s2r, s3s, s3r, r1s, r1r, r2s, r2r, r3s, r3r,
):
    rows, width = tok_in.shape
    chunks = rows // NG
    pairs = width // LANES
    groups = n // GROUP
    scale = 1.0 / math.sqrt(width // H)
    own = BLOCK
    left_at = rows
    right_at = rows + BLOCK
    glob = rows + 2 * BLOCK
    me = lax.axis_index("seq")
    g = me // GROUP
    j = me % GROUP
    base = g * GROUP

    def remote(src, dst, ss, rs, dev):
        return pltpu.make_async_remote_copy(
            src_ref=src, dst_ref=dst, send_sem=ss, recv_sem=rs, device_id=(dev,), device_id_type=MESH
        )

    local = [
        pltpu.make_async_copy(tok_in, tok.at[pl.ds(0, rows)], loc.at[0]),
        pltpu.make_async_copy(wq_in, wq, loc.at[1]),
        pltpu.make_async_copy(wk_in, wk, loc.at[2]),
        pltpu.make_async_copy(wv_in, wv, loc.at[3]),
        pltpu.make_async_copy(wo_in, wo, loc.at[4]),
        pltpu.make_async_copy(gain_in, gain_ref, loc.at[6]),
        pltpu.make_async_copy(bias_in, bias_ref, loc.at[7]),
    ]
    for copy in local[:2]:
        copy.start()

    barrier = pltpu.get_barrier_semaphore()

    def greet(dev):
        pl.semaphore_signal(barrier, inc=1, device_id=(dev,), device_id_type=MESH)

    for d in range(1, GROUP):
        greet(base + (j + d) % GROUP)

    @pl.when(g == 0)
    def _():
        for other in range(1, groups):
            greet(other * GROUP + j)

    @pl.when(g > 0)
    def _():
        greet(jnp.where(j == 0, 1, j))

    has_left = me > 0
    has_right = me < n - 1
    cross_left = (j == 0) & (g > 0)
    cross_right = (j == GROUP - 1) & (g < groups - 1)

    @pl.when(cross_left)
    def _():
        greet(me - 1)

    @pl.when(cross_right)
    def _():
        greet(me + 1)

    column = jnp.where(j == 0, 0, groups - 1) + jnp.where(j == 1, groups - 1, 0)
    peers = GROUP - 1 + jnp.where(g == 0, column, 1) + jnp.where(cross_left, 1, 0) + jnp.where(cross_right, 1, 0)
    pl.semaphore_wait(barrier, peers)

    def glob_piece(index):
        return tok.at[pl.ds(pl.multiple_of(glob + index * PIECE, PIECE), PIECE)]

    wide = pairs // 2 * LANES

    def scatter(d):
        first, count = (0, 2 * PIECE) if d == 1 else (d * PIECE, PIECE)
        return remote(
            tok_in.at[pl.ds(first, count)], tok.at[pl.ds(glob + first, count)], s1s.at[d], s1r.at[0], d
        )

    def glob_half(index, h):
        return tok.at[pl.ds(pl.multiple_of(glob + index * PIECE, PIECE), PIECE), pl.ds(h * wide, wide)]

    def climb(other, h):
        return remote(glob_half(j, h), glob_half(j, h), s2s.at[h, other], s2r.at[h], other * GROUP + j)

    def climb_first(other, h):
        return remote(glob_half(0, h), glob_half(0, h), s2x.at[h, other], s2r.at[h], other * GROUP)

    def gather(h, d):
        t = (j + d) % GROUP
        return remote(glob_half(j, h), glob_half(j, h), s3s.at[h, d], s3r.at[h, d], base + t)

    def gathers(d):
        wanted = (j + d) % GROUP != 0
        if d == 1:
            wanted = wanted & (j > 0)
        return (g > 0) | wanted

    keep = pltpu.make_async_copy(tok_in.at[pl.ds(0, NG)], tok.at[pl.ds(glob, NG)], loc.at[5])

    @pl.when(me == 0)
    def _():
        for d in range(1, GROUP):
            scatter(d).start()
        keep.start()

    to_left = remote(tok_in.at[pl.ds(0, BLOCK)], tok.at[pl.ds(right_at, BLOCK)], halo_s.at[0], halo_r.at[0], me - 1)
    to_right = remote(
        tok_in.at[pl.ds(rows - BLOCK, BLOCK)], tok.at[pl.ds(left_at, BLOCK)], halo_s.at[1], halo_r.at[1], me + 1
    )

    @pl.when(has_left)
    def _():
        to_left.start()

    @pl.when(has_right)
    def _():
        to_right.start()

    for copy in local[2:]:
        copy.start()

    @pl.when(me == 0)
    def _():
        tok[left_at : left_at + BLOCK] = jnp.zeros((BLOCK, width), BF16)

    @pl.when(me == n - 1)
    def _():
        tok[right_at : right_at + BLOCK] = jnp.zeros((BLOCK, width), BF16)

    tile = 2 * LANES if width % (2 * LANES) == 0 else LANES

    def project(w, dst, pieces):
        start, count = pieces[0][0], sum(piece_[2] for piece_ in pieces)
        for t in range(width // tile):
            cols = slice(t * tile, (t + 1) * tile)
            res = jnp.dot(tok[start : start + count], w[:, cols], preferred_element_type=F32).astype(BF16)
            for src, to, size in pieces:
                dst[to : to + size, cols] = res[src - start : src - start + size]

    def project_query(start, count, dst):
        first_half = lax.broadcasted_iota(jnp.int32, (NG, tile), 1) % LANES < BLOCK

        for t in range(width // tile):
            cols = slice(t * tile, (t + 1) * tile)
            res = jnp.dot(tok[start : start + count], wq[:, cols], preferred_element_type=F32) * scale
            for c in range(count // NG):
                part = res[c * NG : (c + 1) * NG]
                dst[2 * c * NG : (2 * c + 1) * NG, cols] = jnp.where(first_half, part, 0.0).astype(BF16)
                dst[(2 * c + 1) * NG : (2 * c + 2) * NG, cols] = jnp.where(first_half, 0.0, part).astype(BF16)

    def gather_sends(h):
        for d in range(1, GROUP):
            @pl.when(gathers(d))
            def _():
                gather(h, d).start()

    @pl.when(g == 0)
    def _():
        @pl.when(j > 1)
        def _():
            remote(glob_piece(j), glob_piece(j), s1s.at[0], s1r.at[0], 0).wait_recv()

        @pl.when(j == 1)
        def _():
            two = tok.at[pl.ds(glob, 2 * PIECE)]
            remote(two, two, s1s.at[0], s1r.at[0], 0).wait_recv()

        @pl.when(j == 0)
        def _():
            keep.wait()

        for h in range(2):
            @pl.when(j > 0)
            def _():
                for other in range(1, groups):
                    climb(other, h).start()

            @pl.when(j == 1)
            def _():
                for other in range(1, groups):
                    climb_first(other, h).start()

        for h in range(2):
            gather_sends(h)

    local[0].wait()
    local[1].wait()
    project_query(0, rows, q)
    local[2].wait()
    project(wk, k, [(0, own, rows)])

    @pl.when(g > 0)
    def _():
        for h in range(2):
            remote(glob_half(j, h), glob_half(j, h), s2s.at[h, 0], s2r.at[h], jnp.where(j == 0, 1, j)).wait_recv()
            gather_sends(h)

    local[3].wait()
    project(wv, v, [(0, own, rows)])

    shape = (2 * NG, NG + 2 * BLOCK)
    row_block = lax.broadcasted_iota(jnp.int32, shape, 0) % NG // BLOCK
    key_id = lax.broadcasted_iota(jnp.int32, shape, 1)
    apart = key_id // BLOCK - row_block
    for c in range(chunks):
        place = me * rows + (c * NG - BLOCK) + key_id
        ok = (apart >= 0) & (apart <= 2) & (place >= NG) & (place < n * rows)
        mask[c] = jnp.where(ok, 0.0, -jnp.inf).astype(F32)

    for d in range(1, GROUP):
        @pl.when(me > (1 if d == 1 else 0))
        def _():
            t = (j + GROUP - d) % GROUP
            for h in range(2):
                remote(glob_half(t, h), glob_half(t, h), s3s.at[h, d], s3r.at[h, d], base + t).wait_recv()

    project_query(glob, NG, qg)

    lane = lax.broadcasted_iota(jnp.int32, (NG, LANES), 1)
    low = lane < BLOCK
    def encode(x):
        hi = x.astype(BF16)
        rest = x - hi.astype(F32)
        mid = rest.astype(BF16)
        lo = (rest - mid.astype(F32)).astype(BF16)
        return (
            hi.astype(F32) + pltpu.roll(mid.astype(F32), 16, 1) + pltpu.roll(lo.astype(F32), 32, 1)
        ).astype(BF16)

    def decode(x):
        x = x.astype(F32)
        return x + pltpu.roll(x, LANES - 16, 1) + pltpu.roll(x, LANES - 32, 1)

    def part(index):
        return pl.ds(pl.multiple_of(index * PIECE, PIECE), PIECE)

    hp = pairs // 2

    def spread(h, d):
        t = (j + d) % GROUP
        return remote(pacc.at[h, part(t)], racc.at[h, d], r1s.at[h, d], r1r.at[h, d], base + t)

    for h in range(2):
        st = jnp.zeros((NG, LANES), F32)
        for i in range(hp):
            cols = slice((h * hp + i) * LANES, (h * hp + i + 1) * LANES)
            s = dot_t(qg[:, cols], k[own : own + rows, cols])
            top = jnp.max(s, axis=-1, keepdims=True)
            e = jnp.exp(s - top)
            total = jnp.sum(e, axis=-1, keepdims=True)
            o = jnp.dot(e.astype(BF16), v[own : own + rows, cols], preferred_element_type=F32)
            pacc[h, :, i * LANES : (i + 1) * LANES] = jnp.where(low, o[:NG], o[NG:]).astype(BF16)
            st = jnp.where(lane == 2 * i, top[:NG], st)
            st = jnp.where(lane == 2 * i + 1, top[NG:], st)
            st = jnp.where(lane == BLOCK + 2 * i, total[:NG], st)
            st = jnp.where(lane == BLOCK + 2 * i + 1, total[NG:], st)
        pacc[h, :, wide:] = encode(st)
        for d in range(1, GROUP):
            spread(h, d).start()
        racc[h, 0] = pacc[h, part(j)]

    small_lane = lax.broadcasted_iota(jnp.int32, (PIECE, LANES), 1)
    small_low = small_lane < BLOCK

    def per_head(x, p, offset):
        return jnp.where(
            small_low, x[:, offset + 2 * p : offset + 2 * p + 1], x[:, offset + 2 * p + 1 : offset + 2 * p + 2]
        )

    def combine(count, accs, h):
        st = [decode(accs[h, d, :, wide:]) for d in range(count)]
        top = functools.reduce(jnp.maximum, st)
        factors = [jnp.exp(s - top) for s in st]
        total = sum(pltpu.roll(f, BLOCK, 1) * s for f, s in zip(factors, st))
        sums = []
        for p in range(hp):
            cols = slice(p * LANES, (p + 1) * LANES)
            sums.append(sum(per_head(factors[d], p, 0) * accs[h, d, :, cols].astype(F32) for d in range(count)))
        st = jnp.where(small_low, top, total)
        return sums, jnp.where(small_lane % BLOCK < 2 * hp, st, 0.0)

    def window(c, p):
        cols = pl.ds(pl.multiple_of(p * LANES, LANES), LANES)
        span = slice(c * NG, c * NG + NG + 2 * BLOCK)
        qs = q[2 * c * NG : 2 * (c + 1) * NG, cols]
        sw = dot_t(qs, k[span, cols]) + mask[c]
        sg = dot_t(qs, k[glob : glob + NG, cols])
        top = jnp.maximum(jnp.max(sw, axis=-1, keepdims=True), jnp.max(sg, axis=-1, keepdims=True))
        ew = jnp.exp(sw - top)
        eg = jnp.exp(sg - top)
        total = jnp.sum(ew, axis=-1, keepdims=True) + jnp.sum(eg, axis=-1, keepdims=True)
        o = jnp.dot(ew.astype(BF16), v[span, cols], preferred_element_type=F32)
        o = o + jnp.dot(eg.astype(BF16), v[glob : glob + NG, cols], preferred_element_type=F32)
        o = o / total
        att[c * NG : (c + 1) * NG, cols] = jnp.where(low, o[:NG], o[NG:]).astype(BF16)

    def windows(c, first, last):
        @pl.loop(first, last, step=2)
        def _(p):
            window(c, p)
            window(c, p + 1)

    def finish(c):
        normalize(c, jnp.dot(att[c * NG : (c + 1) * NG], wo[...], preferred_element_type=F32))

    def normalize(c, proj):
        at = slice(c * NG, (c + 1) * NG)
        summed = tok[c * NG : (c + 1) * NG].astype(F32) + proj
        center = summed - jnp.mean(summed, axis=-1, keepdims=True)
        spread_ = jnp.mean(center * center, axis=-1, keepdims=True)
        out_ref[at] = (center * lax.rsqrt(spread_ + 1e-05) * gain_ref[...][None] + bias_ref[...][None]).astype(BF16)

    @pl.when(has_left)
    def _():
        to_right.wait_recv()

    @pl.when(has_right)
    def _():
        to_left.wait_recv()

    for w, dst in ((wk, k), (wv, v)):
        project(w, dst, [(left_at, 0, BLOCK), (right_at, own + rows, BLOCK), (glob, glob, NG)])


    def raise_up(h):
        return remote(cacc.at[h], zacc.at[h, g], r2s.at[h], r2r.at[h, g], j)

    for h in range(2):
        for d in range(1, GROUP):
            spread(h, d).wait_recv()
        sums, st = combine(GROUP, racc, h)
        sent = [x.astype(BF16) for x in sums] + [encode(st)]

        @pl.when(g == 0)
        def _():
            for p in range(hp + 1):
                zacc[h, 0, :, p * LANES : (p + 1) * LANES] = sent[p]

        @pl.when(g > 0)
        def _():
            for p in range(hp + 1):
                cacc[h, :, p * LANES : (p + 1) * LANES] = sent[p]
            raise_up(h).start()

    for c in range(chunks):
        windows(c, 0, pairs)

    def deliver(h):
        return remote(piece.at[h], gout.at[h, part(j)], r3s.at[h], r3r.at[h, j], 0)

    @pl.when(g == 0)
    def _():
        for h in range(2):
            for other in range(1, groups):
                remote(
                    cacc.at[h], zacc.at[h, other], r2s.at[h], r2r.at[h, other], other * GROUP + j
                ).wait_recv()
            full, full_st = combine(groups, zacc, h)
            for p in range(hp):
                piece[h, :, p * LANES : (p + 1) * LANES] = (full[p] / per_head(full_st, p, BLOCK)).astype(BF16)

            @pl.when(j > 0)
            def _():
                deliver(h).start()

            @pl.when(j == 0)
            def _():
                gout[h, 0:PIECE] = piece[h]

    for copy in local[4:]:
        copy.wait()
    for c in range(1, chunks):
        finish(c)

    @pl.when(me == 0)
    def _():
        proj = jnp.zeros((NG, width), F32)
        for h in range(2):
            for d in range(1, GROUP):
                remote(
                    piece.at[h], gout.at[h, pl.ds(d * PIECE, PIECE)], r3s.at[h], r3r.at[h, d], d
                ).wait_recv()
            proj += jnp.dot(gout[h], wo[h * wide : (h + 1) * wide], preferred_element_type=F32)
        normalize(0, proj)

    @pl.when(me > 0)
    def _():
        finish(0)

    @pl.when(has_left)
    def _():
        to_left.wait_send()

    @pl.when(has_right)
    def _():
        to_right.wait_send()

    @pl.when(me == 0)
    def _():
        for d in range(1, GROUP):
            scatter(d).wait_send()

    @pl.when(g == 0)
    def _():
        @pl.when(j > 0)
        def _():
            for h in range(2):
                for other in range(1, groups):
                    climb(other, h).wait_send()
                deliver(h).wait_send()

        @pl.when(j == 1)
        def _():
            for h in range(2):
                for other in range(1, groups):
                    climb_first(other, h).wait_send()

    @pl.when(g > 0)
    def _():
        for h in range(2):
            raise_up(h).wait_send()

    for d in range(1, GROUP):
        @pl.when(gathers(d))
        def _():
            for h in range(2):
                gather(h, d).wait_send()

        for h in range(2):
            spread(h, d).wait_send()


def shards(n, tokens, w_query, w_key, w_value, w_out, ln_gain, ln_bias):
    rows, width = tokens.shape
    groups = n // GROUP
    ext = rows + 2 * BLOCK + NG
    wide = width // 2
    dma = pltpu.SemaphoreType.DMA
    weight = pltpu.VMEM((width, width), BF16)
    scratch = [
        pltpu.VMEM((ext, width), BF16),
        weight, weight, weight, weight,
        pltpu.VMEM((width,), F32),
        pltpu.VMEM((width,), F32),
        pltpu.VMEM((2 * rows, width), BF16),
        pltpu.VMEM((ext, width), BF16),
        pltpu.VMEM((ext, width), BF16),
        pltpu.VMEM((2 * NG, width), BF16),
        pltpu.VMEM((rows // NG, 2 * NG, NG + 2 * BLOCK), F32),
        pltpu.VMEM((2, NG, wide + LANES), BF16),
        pltpu.VMEM((2, GROUP, PIECE, wide + LANES), BF16),
        pltpu.VMEM((2, PIECE, wide + LANES), BF16),
        pltpu.VMEM((2, groups, PIECE, wide + LANES), BF16),
        pltpu.VMEM((2, PIECE, wide), BF16),
        pltpu.VMEM((2, NG, wide), BF16),
        pltpu.VMEM((rows, width), BF16),
        dma((8,)), dma((2,)), dma((2,)),
        dma((GROUP,)), dma((1,)),
        dma((2, groups)), dma((2, groups)), dma((2,)),
        dma((2, GROUP)), dma((2, GROUP)),
        dma((2, GROUP)), dma((2, GROUP)),
        dma((2,)), dma((2, groups)),
        dma((2,)), dma((2, GROUP)),
    ]
    anywhere = pl.BlockSpec(memory_space=pl.ANY)
    vmem = pl.BlockSpec(memory_space=pltpu.VMEM)
    return pl.pallas_call(
        functools.partial(kernel, n),
        out_shape=jax.ShapeDtypeStruct((rows, width), BF16),
        in_specs=[anywhere] * 7,
        out_specs=vmem,
        scratch_shapes=scratch,
        compiler_params=pltpu.CompilerParams(
            collective_id=0, has_side_effects=True, vmem_limit_bytes=60 * 1024 * 1024
        ),
    )(tokens, w_query, w_key, w_value, w_out, ln_gain, ln_bias)


def solution(mesh):
    n = mesh.shape["seq"]
    in_specs = (P("seq", None), P(), P(), P(), P(), P(), P())
    return jax.shard_map(
        functools.partial(shards, n), mesh=mesh, in_specs=in_specs, out_specs=P("seq", None), check_vma=False
    )
```
